256 devices in a mesh: dp: 128 (over z, y_hi, x, core), mp: 2 (over y_lo).
Axes of the slice: x: 4, y: 4 (y_hi: 2, y_lo: 2; y = y_hi * 2 + y_lo), z: 8, core: 2. Of those that a mesh axis runs over, the one named last changes fastest.
Arguments:
- page_hidden: bfloat16 [256, 1030, 2048], P('dp', 'mp'), may hold values from -24 to 24
- query_hidden: bfloat16 [256, 32, 2048], P('dp', 'mp'), may hold values from -24 to 24
- page_pre: bfloat16 [256, 1030, 128], P('dp')
- query_pre: bfloat16 [256, 32, 128], P('dp')
- match_index: int32 [256, 2, 64], P('dp'), may hold values from 0 to 1029, as said below
- positive: int32 [256], P('dp'), may hold values from 0 to 255, as said below
Outputs:
- d_page_pre: float32 [256, 1030, 128], P('dp', 'mp')
- d_query_pre: float32 [256, 32, 128], P('dp', 'mp')
- grad_weight: float32 [2048, 128], P(('dp', 'mp'))
The draws below stay inside these ranges and needn't reach their ends.
Inputs may be any that keep to these rules, and one draw needn't show every extreme that they name: match_index[c, v, i * 32 + t]: the patch of page c matched to token t of query i of block (c // 2 - v) mod (128). positive[q] lies in block q // 2 or the next block around the cycle.
All inputs are finite; a program needn't handle non-finite values.
Results may differ from the reference program's by a relative error of at most 0.009.
Values may be sent and summed in bfloat16 or wider, within the bound.
No kernel may reach another device: no remote copies, remote signals or barrier semaphores. Data moves between devices by JAX's collectives and lax.ppermute only.
A program may use at most 64 MiB of HBM per device.

```python
import jax
import jax.numpy as jnp
from jax import lax

HID = 2048
EDIM = 128
NP = 1030
QT = 32
PAIRS_DEV = 2
PAGES = 256


def index_table(key):
    return jax.random.randint(jax.random.fold_in(key, 11), (PAGES, 2, PAIRS_DEV * QT), 0, NP, dtype=jnp.int32)


def page_table(key):
    base = jax.random.normal(jax.random.fold_in(key, 12), (PAGES, NP, EDIM), jnp.float32)
    spread = jax.random.uniform(jax.random.fold_in(key, 13), (PAGES, NP, 1), jnp.float32, 0.0, 2.3)
    return base * jnp.exp(spread)


def draw_match_index(key, part):
    return index_table(key)


def draw_page_pre(key, part):
    return page_table(key).astype(jnp.bfloat16)


def draw_query_pre(key, part):
    key = jax.random.fold_in(key, 3)
    noise = jax.random.normal(key, (PAGES, QT, EDIM), jnp.float32)
    return noise.astype(jnp.bfloat16)


def draw_positive(key, part):
    key = jax.random.fold_in(key, 5)
    pick = jax.random.randint(key, (PAGES,), 0, 2 * PAIRS_DEV, dtype=jnp.int32)
    nblock = PAGES // PAIRS_DEV
    block = jnp.arange(PAGES, dtype=jnp.int32) // PAIRS_DEV
    return ((block + pick // PAIRS_DEV) % nblock * PAIRS_DEV + pick % PAIRS_DEV).astype(jnp.int32)


def with_spikes(entries, own_key, source, target, parts, factor):
    def block_of(position):
        return (jnp.arange(entries.shape[position]) // (entries.shape[position] // parts)).reshape((-1,) + (1,) * (entries.ndim - 1 - position))

    first = jax.random.permutation(own_key, parts)[block_of(target)]
    other_side = (block_of(target) + parts // 2) % parts
    return jnp.where((block_of(source) == first) | (block_of(source) == other_side), factor * entries, entries)


def levels(stream_key, shape, cuts, low, top_value):
    factor_of = 1.0
    for axis_at, parts in cuts:
        draws = jax.random.uniform(jax.random.fold_in(jax.random.fold_in(stream_key, 6), axis_at), (parts,), jnp.float32, low / len(cuts), top_value / len(cuts))
        factor_of = factor_of * jnp.repeat(jnp.exp(draws), shape[axis_at] // parts).reshape((-1,) + (1,) * (len(shape) - 1 - axis_at))
    return factor_of


def noise_with(own_key, shape, scale, bound, split, heavy, kind=jnp.bfloat16):
    result = scale * jax.random.normal(own_key, shape, jnp.float32)
    if split:
        result = result * levels(own_key, shape, split, -0.22, 0.18)
    return jnp.clip(with_spikes(result, jax.random.fold_in(own_key, 3), *heavy), -bound, bound).astype(kind)


def setup_inputs(seed: int = 0) -> dict:
    key_of = jax.random.split(jax.random.key(seed), 7)
    page_hidden = noise_with(key_of[0], (PAGES, NP, HID), 1.0, 24.0, ((0, 128), (1, 2)), (0, 2, 128, 5.5))
    query_hidden = noise_with(key_of[1], (PAGES, QT, HID), 1.0, 24.0, ((0, 128), (1, 2)), (0, 2, 128, 5.5))
    page_pre = draw_page_pre(jax.random.fold_in(key_of[6], 71), 0)
    query_pre = draw_query_pre(jax.random.fold_in(key_of[6], 71), 0)
    match_index = draw_match_index(jax.random.fold_in(key_of[6], 71), 0)
    positive = draw_positive(jax.random.fold_in(key_of[6], 71), 0)
    return dict(page_hidden=page_hidden, query_hidden=query_hidden, page_pre=page_pre, query_pre=query_pre, match_index=match_index, positive=positive)


SCALE_LOGIT = 10.0
EPS = 1e-06

def unit_rows(pre):
    pre_wide = pre.astype(jnp.float32)
    norm = jnp.sqrt(lax.optimization_barrier(jnp.sum(pre_wide * pre_wide, axis=-1, keepdims=True)) + EPS)
    return (pre_wide / norm, norm)

def reference(page_hidden, query_hidden, page_pre, query_pre, match_index, positive):
    nblock = PAGES // PAIRS_DEV
    unit_p, norm_p = unit_rows(page_pre)
    unit_q, norm_q = unit_rows(query_pre)
    emb_p = unit_p.astype(jnp.bfloat16)
    emb_q = unit_q.astype(jnp.bfloat16)
    queries = emb_q.astype(jnp.float32).reshape(nblock, PAIRS_DEV, QT, EDIM)
    matched = jax.vmap(lambda table, where: table[where])(emb_p, match_index)
    matched = matched.astype(jnp.float32).reshape(nblock, PAIRS_DEV, 2, PAIRS_DEV, QT, EDIM)
    first = matched[:, :, 0]
    second = jnp.roll(matched[:, :, 1], -1, axis=0)
    score_a = jnp.einsum('bite,bcite->bic', queries, first)
    score_b = jnp.einsum('bite,bcite->bic', queries, second)
    logits = SCALE_LOGIT * jnp.concatenate([score_a, score_b], axis=-1)
    blocks = jnp.arange(nblock, dtype=jnp.int32)[:, None]
    target = positive.reshape(nblock, PAIRS_DEV)
    column = (target // PAIRS_DEV - blocks) % nblock * PAIRS_DEV + target % PAIRS_DEV
    onehot = (column[..., None] == jnp.arange(2 * PAIRS_DEV, dtype=jnp.int32)).astype(jnp.float32)
    probs = jax.nn.softmax(logits, axis=-1)
    grads = (probs - onehot) / PAGES
    grad_a = grads[..., :PAIRS_DEV]
    grad_b = grads[..., PAIRS_DEV:]
    d_emb_q = SCALE_LOGIT * (jnp.einsum('bic,bcite->bite', grad_a, first) + jnp.einsum('bic,bcite->bite', grad_b, second))
    values_a = SCALE_LOGIT * jnp.einsum('bic,bite->bcite', grad_a, queries)
    values_b = jnp.roll(SCALE_LOGIT * jnp.einsum('bic,bite->bcite', grad_b, queries), 1, axis=0)
    values = jnp.stack([values_a, values_b], axis=2).reshape(PAGES, 2 * PAIRS_DEV * QT, EDIM)
    d_emb_p = jax.vmap(lambda where, val: jnp.zeros((NP, EDIM), jnp.float32).at[where].add(val))(match_index.reshape(PAGES, -1), values)
    d_emb_q = d_emb_q.reshape(PAGES, QT, EDIM)
    d_page_pre = (d_emb_p - unit_p * lax.optimization_barrier(jnp.sum(unit_p * d_emb_p, axis=-1, keepdims=True))) / norm_p
    d_query_pre = (d_emb_q - unit_q * lax.optimization_barrier(jnp.sum(unit_q * d_emb_q, axis=-1, keepdims=True))) / norm_q
    low_p = d_page_pre.astype(jnp.bfloat16).reshape(-1, EDIM)
    low_q = d_query_pre.astype(jnp.bfloat16).reshape(-1, EDIM)
    grad_weight = jnp.dot(page_hidden.reshape(-1, HID).T, low_p, preferred_element_type=jnp.float32)
    grad_weight = grad_weight + jnp.dot(query_hidden.reshape(-1, HID).T, low_q, preferred_element_type=jnp.float32)
    return (d_page_pre, d_query_pre, grad_weight)
```

```python
import functools

import jax
import jax.numpy as jnp
from jax import lax
from jax.experimental import pallas as pl
from jax.experimental.pallas import tpu as pltpu
from jax.sharding import Mesh, PartitionSpec as P

SCALE_LOGIT = 10.0
EPS = 1e-06
F32 = jnp.float32
BF16 = jnp.bfloat16


def slot_row(idx_ref, page):
    return jnp.concatenate([idx_ref[page, 0:1, :], idx_ref[page, 1:2, :]], axis=1)


def inverse_norm(wide):
    return lax.rsqrt(jnp.sum(wide * wide, axis=-1, keepdims=True) + EPS)


def rounded_unit(raw):
    wide = raw.astype(F32)
    return (wide * inverse_norm(wide)).astype(BF16).astype(F32)


def gather_kernel(blocks, pos_ref, idx_ref, page_ref, query_ref, first_ref, second_ref, rows_ref):
    per_dev, patches, width = page_ref.shape
    slots = idx_ref.shape[1] * idx_ref.shape[2]
    half = slots // 2
    own, visiting = [], []
    for page in range(per_dev):
        spots = slot_row(idx_ref, page)
        table = (lax.broadcasted_iota(jnp.int32, (patches, slots), 0) == spots).astype(BF16)
        rows = lax.dot_general(
            table, page_ref[page], (((0,), (0,)), ((), ())), preferred_element_type=F32
        ).astype(BF16)
        rows_ref[pl.ds(page * slots, slots), :] = rows
        own.append(rows[:half])
        visiting.append(rows[half:])
    block = lax.axis_index("blk") * 2 + lax.axis_index("core")
    even = lax.axis_index("core") == 0
    lane = lax.broadcasted_iota(jnp.int32, (16, width), 1)
    meta = jnp.zeros((16, width), F32)
    for i in range(per_dev):
        target = pos_ref[i]
        column = (target // per_dev - block + blocks) % blocks * per_dev + target % per_dev
        meta = jnp.where(lane == i, column.astype(F32), meta)
    own = jnp.concatenate(own, axis=0)
    visiting = jnp.concatenate(visiting, axis=0)
    count = own.shape[0]
    first_ref[0:count, :] = jnp.where(even, own, visiting)
    second_ref[0:count, :] = jnp.where(even, visiting, own)
    queries = query_ref[...].reshape(-1, width)
    tail = jnp.concatenate([queries, meta.astype(BF16)], axis=0)
    first_ref[count:, :] = tail
    second_ref[count:, :] = tail


def loss_grads(unit_q, own_rows, other_rows, columns, per_dev, qtokens, pages):
    grads = []
    for i in range(per_dev):
        query = unit_q[i * qtokens : (i + 1) * qtokens]
        scores = []
        for rows in (own_rows, other_rows):
            for c in range(per_dev):
                start = (c * per_dev + i) * qtokens
                prods = jnp.sum(query * rows[start : start + qtokens], axis=0, keepdims=True)
                scores.append(SCALE_LOGIT * jnp.sum(prods, axis=1, keepdims=True))
        top = functools.reduce(jnp.maximum, scores)
        parts = [jnp.exp(s - top) for s in scores]
        total = functools.reduce(jnp.add, parts)
        grads.append(
            [
                (part / total - (columns[i] == j).astype(F32)) * (SCALE_LOGIT / pages)
                for j, part in enumerate(parts)
            ]
        )
    return grads


def main_kernel(
    pages, pos_ref, idx_ref, first_ref, second_ref, rows_ref, query_ref, half_ref, qhid_ref, hid_ref,
    d_page_ref, d_query_ref, send_ref, keep_ref, hid, sem,
):
    per_dev, patches, width = half_ref.shape
    slots = idx_ref.shape[1] * idx_ref.shape[2]
    half = slots // 2
    qtokens = query_ref.shape[1]
    tokens = qhid_ref.shape[1]
    copies = [pltpu.make_async_copy(hid_ref.at[c], hid.at[c], sem.at[c]) for c in range(per_dev)]
    for copy in copies:
        copy.start()
    blocks = pages // per_dev
    core = lax.axis_index("core")
    split = lax.axis_index("mp")
    block = lax.axis_index("blk") * 2 + core
    even = core == 0
    count = per_dev * half
    qcount = per_dev * qtokens

    first, second = first_ref[...], second_ref[...]
    after = jnp.where(even, first[:count], second[:count])
    before = jnp.where(even, second, first)
    own_unit = rounded_unit(jnp.concatenate([rows_ref[c * slots : c * slots + half] for c in range(per_dev)], axis=0))
    visit_unit = rounded_unit(
        jnp.concatenate([rows_ref[c * slots + half : (c + 1) * slots] for c in range(per_dev)], axis=0)
    )
    after_unit = rounded_unit(after)
    before_rows = rounded_unit(before[:count])
    before_q = rounded_unit(before[count : count + qcount])
    q_wide = query_ref[...].reshape(qcount, width).astype(F32)
    q_inv = inverse_norm(q_wide)
    q_unit = q_wide * q_inv
    q_low = q_unit.astype(BF16).astype(F32)

    columns = []
    for i in range(per_dev):
        target = pos_ref[i]
        columns.append(
            jnp.full((1, 1), (target // per_dev - block + blocks) % blocks * per_dev + target % per_dev).astype(F32)
        )
    meta = before[count + qcount :].astype(F32)
    before_columns = [meta[0:1, i : i + 1] for i in range(per_dev)]
    grads = loss_grads(q_low, own_unit, after_unit, columns, per_dev, qtokens, pages)
    before_grads = loss_grads(before_q, before_rows, visit_unit, before_columns, per_dev, qtokens, pages)

    low_q = []
    for i in range(per_dev):
        wide = jnp.zeros((qtokens, width), F32)
        for c in range(per_dev):
            start = (c * per_dev + i) * qtokens
            wide += grads[i][c] * own_unit[start : start + qtokens]
            wide += grads[i][per_dev + c] * after_unit[start : start + qtokens]
        unit = q_unit[i * qtokens : (i + 1) * qtokens]
        out = (wide - unit * jnp.sum(unit * wide, axis=-1, keepdims=True)) * q_inv[i * qtokens : (i + 1) * qtokens]
        out = jnp.where(split == 0, out[:tokens], out[tokens:])
        d_query_ref[i] = out
        low_q.append(out.astype(BF16))

    low_p = []
    for c in range(per_dev):
        values = jnp.concatenate(
            [grads[i][c] * q_low[i * qtokens : (i + 1) * qtokens] for i in range(per_dev)]
            + [before_grads[i][per_dev + c] * before_q[i * qtokens : (i + 1) * qtokens] for i in range(per_dev)],
            axis=0,
        )
        high = values.astype(BF16)
        rest = (values - high.astype(F32)).astype(BF16)
        spots = slot_row(idx_ref, c) - split * patches
        table = (lax.broadcasted_iota(jnp.int32, (patches, slots), 0) == spots).astype(BF16)
        both = jnp.dot(table, jnp.concatenate([high, rest], axis=1), preferred_element_type=F32)
        wide = both[:, :width] + both[:, width:]
        page = half_ref[c].astype(F32)
        inv = inverse_norm(page)
        unit = page * inv
        out = (wide - unit * jnp.sum(unit * wide, axis=-1, keepdims=True)) * inv
        d_page_ref[c] = out
        low_p.append(out.astype(BF16))

    dims = (((0,), (0,)), ((), ()))
    total = jnp.zeros((width, qhid_ref.shape[2]), F32)
    for i in range(per_dev):
        total += lax.dot_general(low_q[i], qhid_ref[i], dims, preferred_element_type=F32)
    for c in range(per_dev):
        copies[c].wait()
        total += lax.dot_general(low_p[c], hid[c], dims, preferred_element_type=F32)
    groups, rows = keep_ref.shape[0], keep_ref.shape[1]
    partial = total.T.reshape(groups, 2, rows, width)
    keep_ref[...] = jnp.where(even, partial[:, 0], partial[:, 1])
    send_ref[...] = jnp.where(even, partial[:, 1], partial[:, 0]).astype(BF16)


def shards(page_hidden, query_hidden, page_pre, query_pre, match_index, positive):
    per_dev, _, width = page_pre.shape
    qtokens = query_pre.shape[1]
    patches = page_hidden.shape[1]
    hidden = page_hidden.shape[2]
    groups = lax.axis_size("blk")
    blocks = groups * 2
    pages = blocks * per_dev
    slots = match_index.shape[1] * match_index.shape[2]
    split = lax.axis_index("mp")
    vmem = pl.BlockSpec(memory_space=pltpu.VMEM)
    smem = pl.BlockSpec(memory_space=pltpu.SMEM)
    count = per_dev * (slots // 2) + per_dev * qtokens + 16
    payload = jax.ShapeDtypeStruct((count, width), BF16)
    first, second, rows = pl.pallas_call(
        functools.partial(gather_kernel, blocks),
        out_shape=(payload, payload, jax.ShapeDtypeStruct((per_dev * slots, width), BF16)),
        in_specs=[smem, vmem, vmem, vmem],
        out_specs=(vmem, vmem, vmem),
        compiler_params=pltpu.CompilerParams(vmem_limit_bytes=32 * 2**20),
        name="gather_rows",
    )(positive, match_index, page_pre, query_pre)
    swap = [(i, i ^ 1) for i in range(blocks)]
    cross = [(i, (i + 1) % blocks if i % 2 else (i - 1) % blocks) for i in range(blocks)]
    second = lax.ppermute(second, ("blk", "core"), cross)
    first = lax.ppermute(first, ("blk", "core"), swap)
    half = lax.dynamic_slice_in_dim(page_pre, split * patches, patches, 1)
    share = hidden // (2 * groups)
    d_page, d_query, send, keep = pl.pallas_call(
        functools.partial(main_kernel, pages),
        out_shape=(
            jax.ShapeDtypeStruct((per_dev, patches, width), F32),
            jax.ShapeDtypeStruct((per_dev, query_hidden.shape[1], width), F32),
            jax.ShapeDtypeStruct((groups, share, width), BF16),
            jax.ShapeDtypeStruct((groups, share, width), F32),
        ),
        in_specs=[smem] + [vmem] * 7 + [pl.BlockSpec(memory_space=pl.ANY)],
        out_specs=(vmem, vmem, vmem, vmem),
        scratch_shapes=[pltpu.VMEM(page_hidden.shape, BF16), pltpu.SemaphoreType.DMA((per_dev,))],
        compiler_params=pltpu.CompilerParams(vmem_limit_bytes=48 * 2**20),
        name="grads_and_partial",
    )(positive, match_index, first, second, rows, query_pre, half, query_hidden, page_hidden)
    got = lax.ppermute(send, "core", [(0, 1), (1, 0)])
    pair = (keep + got.astype(F32)).astype(BF16).reshape(groups * 2, share // 2, width)
    parts = lax.all_to_all(pair, ("blk", "mp"), 0, 0, tiled=True)
    return d_page, d_query, jnp.sum(parts.astype(F32), axis=0)


def solution(mesh):
    blocks, parts = mesh.devices.shape
    fine = Mesh(mesh.devices.reshape(blocks // 2, 2, parts), ("blk", "core", "mp"))
    dp = ("blk", "core")
    placed = (
        P(dp, "mp", None),
        P(dp, "mp", None),
        P(dp, None, None),
        P(dp, None, None),
        P(dp, None, None),
        P(dp),
    )
    return jax.shard_map(
        shards,
        mesh=fine,
        in_specs=placed,
        out_specs=(P(dp, "mp", None), P(dp, "mp", None), P(("blk", "core", "mp"), None)),
        check_vma=False,
    )
```

```python
import functools

import jax
import jax.numpy as jnp
from jax import lax
from jax.experimental import pallas as pl
from jax.experimental.pallas import tpu as pltpu
from jax.sharding import Mesh, PartitionSpec as P

SCALE_LOGIT = 10.0
EPS = 1e-06
F32 = jnp.float32
BF16 = jnp.bfloat16
LANES = 128
RUN = 4
VMEM = pl.BlockSpec(memory_space=pltpu.VMEM)
ANY = pl.BlockSpec(memory_space=pl.ANY)


def one_hot(targets, rows):
    return (lax.broadcasted_iota(jnp.int32, (rows, targets.shape[1]), 0) == targets).astype(BF16)


def inverse_norm(wide):
    return lax.rsqrt(jnp.sum(wide * wide, axis=-1, keepdims=True) + EPS)


def rounded(wide):
    return wide.astype(BF16).astype(F32)


def rounded_unit(raw):
    wide = raw.astype(F32)
    return rounded(wide * inverse_norm(wide))


def place_kernel(out_ref):
    block = lax.axis_index("blk") * 2 + lax.axis_index("core")
    out_ref[...] = jnp.full(out_ref.shape, block, jnp.int32)


def gather_kernel(blocks, place_ref, idx_ref, pos_ref, query_ref, page_ref, first_ref, second_ref, rows_ref, half_ref, misc_ref):
    patches, per_dev, width = page_ref.shape
    flat = patches * per_dev
    half = idx_ref.shape[2]
    spots = jnp.concatenate(
        [idx_ref[c, v : v + 1, :] * per_dev + c for c in range(per_dev) for v in range(idx_ref.shape[1])], axis=1
    )
    target = pos_ref[...]
    rows = lax.dot_general(
        one_hot(spots, flat),
        page_ref[...].reshape(flat, width),
        (((0,), (0,)), ((), ())),
        preferred_element_type=F32,
    ).astype(BF16)
    rows_ref[...] = rows
    own = jnp.concatenate([rows[2 * c * half : (2 * c + 1) * half] for c in range(per_dev)], axis=0)
    visiting = jnp.concatenate([rows[(2 * c + 1) * half : (2 * c + 2) * half] for c in range(per_dev)], axis=0)
    even = lax.axis_index("core") == 0
    shift = target // per_dev - place_ref[0:1, :per_dev] + blocks
    column = jnp.where(shift >= blocks, shift - blocks, shift) * per_dev + target % per_dev
    count = own.shape[0]
    first_ref[0:count, :] = jnp.where(even, own, visiting)
    second_ref[0:count, :] = jnp.where(even, visiting, own)
    lane = lax.broadcasted_iota(jnp.int32, (16, width), 1)
    meta = jnp.zeros((16, width), F32)
    for i in range(per_dev):
        meta = jnp.where(lane == i, column[:, i : i + 1].astype(F32), meta)
    tail = jnp.concatenate([query_ref[...].reshape(-1, width), meta.astype(BF16)], axis=0)
    first_ref[count:, :] = tail
    second_ref[count:, :] = tail
    half_rows = half_ref.shape[0]
    start = lax.axis_index("mp") * half_rows
    half_ref[...] = page_ref[pl.ds(start, half_rows)]
    misc_ref[...] = jnp.broadcast_to(spots - start * per_dev, misc_ref.shape)


def local_kernel(
    sent_ref, rows_ref, half_ref, misc_ref, hid_ref, unit_ref, inv_ref, table_ref, own_ref, visit_ref, query_ref,
    qinv_ref, slot_unit_ref, slot_inv_ref, same_ref, picked_ref,
):
    patches, per_dev, width = half_ref.shape
    flat = patches * per_dev
    slots = rows_ref.shape[0]
    half = slots // (2 * per_dev)
    spots = misc_ref[0:1, :]
    table = one_hot(spots, flat)
    table_ref[...] = table
    page = half_ref[...].reshape(flat, width).astype(F32)
    inv = inverse_norm(page)
    unit_ref[...] = page * inv
    inv_ref[...] = jnp.broadcast_to(inv, (flat, width))
    wide = rows_ref[...].astype(F32)
    inv = inverse_norm(wide)
    slot_unit = wide * inv
    slot_unit_ref[...] = slot_unit
    for c in range(per_dev):
        own_ref[c * half : (c + 1) * half] = rounded(slot_unit[2 * c * half : (2 * c + 1) * half])
        visit_ref[c * half : (c + 1) * half] = rounded(slot_unit[(2 * c + 1) * half : (2 * c + 2) * half])
    column = misc_ref[...].astype(F32).T[:, 0:1]
    same = column == spots.astype(F32)
    earlier = lax.broadcasted_iota(jnp.int32, same.shape, 1) < lax.broadcasted_iota(jnp.int32, same.shape, 0)
    repeats = jnp.sum((same & earlier).astype(F32), axis=1, keepdims=True)
    counts = (repeats == 0) & (column >= 0) & (column < flat)
    same_ref[...] = same.astype(BF16)
    slot_inv_ref[...] = jnp.where(counts, inv, 0.0) + jnp.zeros((slots, width), F32)
    wide = sent_ref[per_dev * half : (per_dev + 1) * half, :].astype(F32)
    inv = inverse_norm(wide)
    query_ref[...] = wide * inv
    qinv_ref[...] = jnp.broadcast_to(inv, wide.shape)
    picked_ref[...] = lax.dot_general(
        table, hid_ref[...].reshape(flat, -1), (((0,), (0,)), ((), ())), preferred_element_type=F32
    ).astype(BF16)


def loss_grads(unit_q, own_rows, other_rows, columns, per_dev, qtokens, pages):
    grads = []
    for i in range(per_dev):
        query = unit_q[i * qtokens : (i + 1) * qtokens]
        scores = []
        for rows in (own_rows, other_rows):
            for c in range(per_dev):
                start = (c * per_dev + i) * qtokens
                prods = jnp.sum(query * rows[start : start + qtokens], axis=0, keepdims=True)
                scores.append(SCALE_LOGIT * jnp.sum(prods, axis=1, keepdims=True))
        top = functools.reduce(jnp.maximum, scores)
        parts = [jnp.exp(s - top) for s in scores]
        total = functools.reduce(jnp.add, parts)
        grads.append(
            [
                (part / total - (columns[i] == j).astype(F32)) * (SCALE_LOGIT / pages)
                for j, part in enumerate(parts)
            ]
        )
    return grads


def main_kernel(
    pages, per_dev, sent_ref, first_ref, second_ref, own_ref, visit_ref, query_ref, qinv_ref, slot_unit_ref,
    slot_inv_ref, same_ref, picked_ref, qhid_ref, d_query_ref, values_ref, send_ref, keep_ref,
):
    qcount, width = query_ref.shape
    qtokens = qcount // per_dev
    tokens = qhid_ref.shape[1]
    split = lax.axis_index("mp")
    even = lax.axis_index("core") == 0
    count = own_ref.shape[0]

    first, second = first_ref[...], second_ref[...]
    after = jnp.where(even, first[:count], second[:count])
    before = jnp.where(even, second, first)
    own_unit = own_ref[...]
    visit_unit = visit_ref[...]
    after_unit = rounded_unit(after)
    before_rows = rounded_unit(before[:count])
    before_q = rounded_unit(before[count : count + qcount])
    q_unit = query_ref[...]
    q_inv = qinv_ref[...]
    q_low = q_unit.astype(BF16).astype(F32)

    own_meta = sent_ref[count + qcount :, :].astype(F32)
    before_meta = before[count + qcount :].astype(F32)
    columns = [own_meta[0:1, i : i + 1] for i in range(per_dev)]
    before_columns = [before_meta[0:1, i : i + 1] for i in range(per_dev)]
    grads = loss_grads(q_low, own_unit, after_unit, columns, per_dev, qtokens, pages)
    before_grads = loss_grads(before_q, before_rows, visit_unit, before_columns, per_dev, qtokens, pages)

    values = []
    for c in range(per_dev):
        for i in range(per_dev):
            values.append(grads[i][c] * q_low[i * qtokens : (i + 1) * qtokens])
        for i in range(per_dev):
            values.append(before_grads[i][per_dev + c] * before_q[i * qtokens : (i + 1) * qtokens])
    values = jnp.concatenate(values, axis=0)
    high = values.astype(BF16)
    rest = (values - high.astype(F32)).astype(BF16)
    parts = jnp.concatenate([high, rest], axis=1)
    values_ref[...] = parts
    both = jnp.dot(same_ref[...], parts, preferred_element_type=F32)
    wide = both[:, :width] + both[:, width:]
    unit = slot_unit_ref[...]
    out = (wide - unit * jnp.sum(unit * wide, axis=-1, keepdims=True)) * slot_inv_ref[...]

    low = []
    for i in range(per_dev):
        wide_q = jnp.zeros((qtokens, width), F32)
        for c in range(per_dev):
            start = (c * per_dev + i) * qtokens
            wide_q += grads[i][c] * own_unit[start : start + qtokens]
            wide_q += grads[i][per_dev + c] * after_unit[start : start + qtokens]
        unit_i = q_unit[i * qtokens : (i + 1) * qtokens]
        out_q = (wide_q - unit_i * jnp.sum(unit_i * wide_q, axis=-1, keepdims=True)) * q_inv[
            i * qtokens : (i + 1) * qtokens
        ]
        out_q = jnp.where(split == 0, out_q[:tokens], out_q[tokens:])
        d_query_ref[i] = out_q
        low.append(out_q)
    low = jnp.concatenate(low, axis=0)
    total = jnp.dot(out.T.astype(BF16), picked_ref[...], preferred_element_type=F32)
    total += jnp.dot(
        low.T.astype(BF16), qhid_ref[...].reshape(per_dev * tokens, -1), preferred_element_type=F32
    )
    rows = keep_ref.shape[1]
    step = LANES // (2 * rows)
    for t in range(total.shape[1] // LANES):
        part = total[:, t * LANES : (t + 1) * LANES].T.reshape(step, 2, rows, width)
        keep_ref[t * step : (t + 1) * step] = jnp.where(even, part[:, 0], part[:, 1])
        send_ref[t * step : (t + 1) * step] = jnp.where(even, part[:, 1], part[:, 0]).astype(BF16)


def page_kernel(values_ref, table_ref, unit_ref, inv_ref, _keep_in, out_ref, _keep_out):
    width = unit_ref.shape[1]
    both = jnp.dot(table_ref[...], values_ref[...], preferred_element_type=F32)
    wide = both[:, :width] + both[:, width:]
    unit = unit_ref[...]
    out = (wide - unit * jnp.sum(unit * wide, axis=-1, keepdims=True)) * inv_ref[...]
    out_ref[...] = out.reshape(out_ref.shape)


def add_kernel(keep_ref, got_ref, out_ref):
    out_ref[...] = (keep_ref[...] + got_ref[...].astype(F32)).astype(BF16)


def sum_kernel(parts_ref, out_ref):
    total = jnp.sum(parts_ref[...].astype(F32), axis=0)
    rows = out_ref.shape[0]
    out_ref[...] = total[:rows] + total[rows:]


def shards(page_hidden, query_hidden, page_pre, query_pre, match_index, positive):
    per_dev, patches_all, width = page_pre.shape
    qtokens = query_pre.shape[1]
    patches = page_hidden.shape[1]
    hidden = page_hidden.shape[2]
    groups = lax.axis_size("blk")
    blocks = groups * 2
    pages = blocks * per_dev
    slots = per_dev * match_index.shape[1] * match_index.shape[2]
    page_t = jnp.transpose(page_pre, (1, 0, 2))
    hid_t = jnp.transpose(page_hidden, (1, 0, 2))
    limit = pltpu.CompilerParams(vmem_limit_bytes=24 * 2**20)
    place = pl.pallas_call(
        place_kernel,
        out_shape=jax.ShapeDtypeStruct((8, LANES), jnp.int32),
        out_specs=VMEM,
        compiler_params=limit,
        cost_estimate=pl.CostEstimate(flops=5 * 10**9, bytes_accessed=4096, transcendentals=0),
        name="place",
    )()
    count = slots // 2 + per_dev * qtokens + 16
    payload = jax.ShapeDtypeStruct((count, width), BF16)
    first, second, rows, half, misc = pl.pallas_call(
        functools.partial(gather_kernel, blocks),
        out_shape=(
            payload,
            payload,
            jax.ShapeDtypeStruct((slots, width), BF16),
            jax.ShapeDtypeStruct((patches, per_dev, width), BF16),
            jax.ShapeDtypeStruct((8, slots), jnp.int32),
        ),
        in_specs=[VMEM] * 5,
        out_specs=(VMEM,) * 5,
        compiler_params=limit,
        name="gather_rows",
    )(place, match_index, positive.reshape(1, per_dev), query_pre, page_t)
    swap = [(i, i ^ 1) for i in range(blocks)]
    cross = []
    for i in range(blocks):
        j = (i + 1) % blocks if i % 2 else (i - 1) % blocks
        for part in range(lax.axis_size("mp")):
            cross.append((2 * i + part, 2 * j + (part if i // (2 * RUN) == j // (2 * RUN) else 1 - part)))
    far = lax.ppermute(second, ("blk", "core", "mp"), cross)
    near = lax.ppermute(first, ("blk", "core"), swap)
    wide_rows = jax.ShapeDtypeStruct((patches * per_dev, width), F32)
    own_rows = jax.ShapeDtypeStruct((slots // 2, width), F32)
    own_queries = jax.ShapeDtypeStruct((per_dev * qtokens, width), F32)
    slot_rows = jax.ShapeDtypeStruct((slots, width), F32)
    unit, inv, table, *local = pl.pallas_call(
        local_kernel,
        out_shape=(
            wide_rows,
            wide_rows,
            jax.ShapeDtypeStruct((patches * per_dev, slots), BF16),
            own_rows,
            own_rows,
            own_queries,
            own_queries,
            slot_rows,
            slot_rows,
            jax.ShapeDtypeStruct((slots, slots), BF16),
            jax.ShapeDtypeStruct((slots, hidden), BF16),
        ),
        in_specs=[VMEM] * 5,
        out_specs=(VMEM,) * 11,
        compiler_params=limit,
        cost_estimate=pl.CostEstimate(flops=5 * 10**9, bytes_accessed=10**6, transcendentals=0),
        name="local_rows",
    )(first, rows, half, misc, hid_t)
    share = hidden // (2 * groups)
    d_query, values, send, keep = pl.pallas_call(
        functools.partial(main_kernel, pages, per_dev),
        out_shape=(
            jax.ShapeDtypeStruct((per_dev, query_hidden.shape[1], width), F32),
            jax.ShapeDtypeStruct((slots, 2 * width), BF16),
            jax.ShapeDtypeStruct((groups, share, width), BF16),
            jax.ShapeDtypeStruct((groups, share, width), F32),
        ),
        in_specs=[VMEM] * 12,
        out_specs=(VMEM,) * 4,
        compiler_params=limit,
        name="grads_and_partial",
    )(first, near, far, *local, query_hidden)
    got = lax.ppermute(send, "core", [(0, 1), (1, 0)])
    d_page, keep = pl.pallas_call(
        page_kernel,
        out_shape=(jax.ShapeDtypeStruct((patches, per_dev, width), F32), jax.ShapeDtypeStruct(keep.shape, F32)),
        in_specs=[VMEM] * 4 + [ANY],
        out_specs=(VMEM, ANY),
        input_output_aliases={4: 1},
        compiler_params=limit,
        cost_estimate=pl.CostEstimate(flops=10**9, bytes_accessed=10**6, transcendentals=0),
        name="page_grads",
    )(values, table, unit, inv, keep)
    small = pltpu.CompilerParams(vmem_limit_bytes=16 * 2**20)
    pair = pl.pallas_call(
        add_kernel,
        out_shape=jax.ShapeDtypeStruct(got.shape, BF16),
        in_specs=[VMEM, VMEM],
        out_specs=VMEM,
        compiler_params=small,
        name="add_pair",
    )(keep, got)
    parts = lax.all_to_all(pair.reshape(groups * 2, share // 2, width), ("blk", "mp"), 0, 0, tiled=True)
    grad = pl.pallas_call(
        sum_kernel,
        out_shape=jax.ShapeDtypeStruct((share // 2, width), F32),
        in_specs=[VMEM],
        out_specs=VMEM,
        compiler_params=small,
        name="sum_parts",
    )(parts.reshape(groups, share, width))
    return jnp.transpose(d_page, (1, 0, 2)), d_query, grad


def solution(mesh):
    blocks, parts = mesh.devices.shape
    fine = Mesh(mesh.devices.reshape(blocks // 2, 2, parts), ("blk", "core", "mp"))
    dp = ("blk", "core")
    placed = (
        P(dp, "mp", None),
        P(dp, "mp", None),
        P(dp, None, None),
        P(dp, None, None),
        P(dp, None, None),
        P(dp),
    )
    return jax.shard_map(
        shards,
        mesh=fine,
        in_specs=placed,
        out_specs=(P(dp, "mp", None), P(dp, "mp", None), P(("blk", "core", "mp"), None)),
        check_vma=False,
    )
```

```python
import functools

import jax
import jax.numpy as jnp
from jax import lax
from jax.experimental import pallas as pl
from jax.experimental.pallas import tpu as pltpu
from jax.sharding import Mesh, PartitionSpec as P

SCALE_LOGIT = 10.0
EPS = 1e-06
F32 = jnp.float32
BF16 = jnp.bfloat16
LANES = 128
RUN = 4
PLANES = 8
BLK = ("z2", "z1", "z0", "run")
DP = BLK + ("core",)
VMEM = pl.BlockSpec(memory_space=pltpu.VMEM)
ANY = pl.BlockSpec(memory_space=pl.ANY)


def one_hot(targets, rows):
    at = lax.broadcasted_iota(jnp.int16, (rows, targets.shape[1]), 0)
    return jnp.where(at == targets.astype(jnp.int16), jnp.ones((), BF16), jnp.zeros((), BF16))


def inverse_norm(wide):
    return lax.rsqrt(jnp.sum(wide * wide, axis=-1, keepdims=True) + EPS)


def rounded(wide):
    return wide.astype(BF16).astype(F32)


def rounded_unit(raw):
    wide = raw.astype(F32)
    return rounded(wide * inverse_norm(wide))


def place_kernel(out_ref):
    block = lax.axis_index(DP)
    out_ref[...] = jnp.full(out_ref.shape, block, jnp.int32)


def gather_kernel(blocks, place_ref, idx_ref, pos_ref, query_ref, page_ref, first_ref, second_ref, rows_ref, half_ref, misc_ref):
    patches, per_dev, width = page_ref.shape
    flat = patches * per_dev
    half = idx_ref.shape[2]
    spots = jnp.concatenate(
        [idx_ref[c, v : v + 1, :] * per_dev + c for c in range(per_dev) for v in range(idx_ref.shape[1])], axis=1
    )
    target = pos_ref[...]
    rows = lax.dot_general(
        one_hot(spots, flat),
        page_ref[...].reshape(flat, width),
        (((0,), (0,)), ((), ())),
        preferred_element_type=F32,
    ).astype(BF16)
    rows_ref[...] = rows
    own = jnp.concatenate([rows[2 * c * half : (2 * c + 1) * half] for c in range(per_dev)], axis=0)
    visiting = jnp.concatenate([rows[(2 * c + 1) * half : (2 * c + 2) * half] for c in range(per_dev)], axis=0)
    even = lax.axis_index("core") == 0
    shift = target // per_dev - place_ref[0:1, :per_dev] + blocks
    column = jnp.where(shift >= blocks, shift - blocks, shift) * per_dev + target % per_dev
    count = own.shape[0]
    first_ref[0:count, :] = jnp.where(even, own, visiting)
    second_ref[0:count, :] = jnp.where(even, visiting, own)
    lane = lax.broadcasted_iota(jnp.int32, (16, width), 1)
    meta = jnp.zeros((16, width), F32)
    for i in range(per_dev):
        meta = jnp.where(lane == i, column[:, i : i + 1].astype(F32), meta)
    tail = jnp.concatenate([query_ref[...].reshape(-1, width), meta.astype(BF16)], axis=0)
    first_ref[count:, :] = tail
    second_ref[count:, :] = tail
    half_rows = half_ref.shape[0]
    start = lax.axis_index("mp") * half_rows
    half_ref[...] = page_ref[pl.ds(start, half_rows)]
    misc_ref[...] = jnp.broadcast_to(spots - start * per_dev, misc_ref.shape)


def local_kernel(
    sent_ref, rows_ref, half_ref, misc_ref, hid_ref, qhid_ref, unit_ref, inv_ref, table_ref, own_ref, visit_ref, query_ref,
    qinv_ref, slot_unit_ref, slot_inv_ref, same_ref, there_ref, here_ref,
):
    patches, per_dev, width = half_ref.shape
    flat = patches * per_dev
    slots = rows_ref.shape[0]
    half = slots // (2 * per_dev)
    spots = misc_ref[0:1, :]
    table = one_hot(spots, flat)
    table_ref[...] = table
    page = half_ref[...].reshape(flat, width).astype(F32)
    inv = inverse_norm(page)
    unit_ref[...] = page * inv
    inv_ref[...] = jnp.broadcast_to(inv, (flat, width))
    wide = rows_ref[...].astype(F32)
    inv = inverse_norm(wide)
    slot_unit = wide * inv
    slot_unit_ref[...] = slot_unit
    for c in range(per_dev):
        own_ref[c * half : (c + 1) * half] = rounded(slot_unit[2 * c * half : (2 * c + 1) * half])
        visit_ref[c * half : (c + 1) * half] = rounded(slot_unit[(2 * c + 1) * half : (2 * c + 2) * half])
    column = misc_ref[...].astype(F32).T[:, 0:1]
    same = column == spots.astype(F32)
    earlier = lax.broadcasted_iota(jnp.int32, same.shape, 1) < lax.broadcasted_iota(jnp.int32, same.shape, 0)
    repeats = jnp.sum((same & earlier).astype(F32), axis=1, keepdims=True)
    counts = (repeats == 0) & (column >= 0) & (column < flat)
    same_ref[...] = same.astype(BF16)
    slot_inv_ref[...] = jnp.where(counts, inv, 0.0) + jnp.zeros((slots, width), F32)
    wide = sent_ref[per_dev * half : (per_dev + 1) * half, :].astype(F32)
    inv = inverse_norm(wide)
    query_ref[...] = wide * inv
    qinv_ref[...] = jnp.broadcast_to(inv, wide.shape)
    dims = (((0,), (0,)), ((), ()))
    tokens = qhid_ref.shape[0] * qhid_ref.shape[1]
    eye = one_hot(lax.broadcasted_iota(jnp.int32, (1, tokens), 1), tokens)
    picked = lax.dot_general(hid_ref[...].reshape(flat, -1), table, dims, preferred_element_type=F32)
    turned = lax.dot_general(qhid_ref[...].reshape(tokens, -1), eye, dims, preferred_element_type=F32)
    even = lax.axis_index("core") == 0
    groups, share, _ = here_ref.shape
    for part, at in ((picked, slice(0, slots)), (turned, slice(slots, slots + tokens))):
        part = part.astype(BF16).reshape(groups, 2, share, part.shape[1])
        here_ref[:, :, at] = jnp.where(even, part[:, 0], part[:, 1])
        there_ref[:, :, at] = jnp.where(even, part[:, 1], part[:, 0])


def loss_grads(unit_q, own_rows, other_rows, columns, per_dev, qtokens, pages):
    grads = []
    for i in range(per_dev):
        query = unit_q[i * qtokens : (i + 1) * qtokens]
        scores = []
        for rows in (own_rows, other_rows):
            for c in range(per_dev):
                start = (c * per_dev + i) * qtokens
                prods = jnp.sum(query * rows[start : start + qtokens], axis=0, keepdims=True)
                scores.append(SCALE_LOGIT * jnp.sum(prods, axis=1, keepdims=True))
        top = functools.reduce(jnp.maximum, scores)
        parts = [jnp.exp(s - top) for s in scores]
        total = functools.reduce(jnp.add, parts)
        grads.append(
            [
                (part / total - (columns[i] == j).astype(F32)) * (SCALE_LOGIT / pages)
                for j, part in enumerate(parts)
            ]
        )
    return grads


def partial_sum(hid_ref, low):
    groups, share, depth = hid_ref.shape
    total = jnp.dot(hid_ref[...].reshape(groups * share, depth), low, preferred_element_type=F32)
    return total.reshape(groups, share, low.shape[1])


def main_kernel(
    pages, per_dev, sent_ref, first_ref, second_ref, own_ref, visit_ref, query_ref, qinv_ref, slot_unit_ref,
    slot_inv_ref, same_ref, there_ref, d_query_ref, values_ref, low_ref, send_ref,
):
    qcount, width = query_ref.shape
    qtokens = qcount // per_dev
    tokens = d_query_ref.shape[1]
    split = lax.axis_index("mp")
    even = lax.axis_index("core") == 0
    count = own_ref.shape[0]

    first, second = first_ref[...], second_ref[...]
    after = jnp.where(even, first[:count], second[:count])
    before = jnp.where(even, second, first)
    own_unit = own_ref[...]
    visit_unit = visit_ref[...]
    after_unit = rounded_unit(after)
    before_rows = rounded_unit(before[:count])
    before_q = rounded_unit(before[count : count + qcount])
    q_unit = query_ref[...]
    q_inv = qinv_ref[...]
    q_low = q_unit.astype(BF16).astype(F32)

    own_meta = sent_ref[count + qcount :, :].astype(F32)
    before_meta = before[count + qcount :].astype(F32)
    columns = [own_meta[0:1, i : i + 1] for i in range(per_dev)]
    before_columns = [before_meta[0:1, i : i + 1] for i in range(per_dev)]
    grads = loss_grads(q_low, own_unit, after_unit, columns, per_dev, qtokens, pages)
    before_grads = loss_grads(before_q, before_rows, visit_unit, before_columns, per_dev, qtokens, pages)

    values = []
    for c in range(per_dev):
        for i in range(per_dev):
            values.append(grads[i][c] * q_low[i * qtokens : (i + 1) * qtokens])
        for i in range(per_dev):
            values.append(before_grads[i][per_dev + c] * before_q[i * qtokens : (i + 1) * qtokens])
    values = jnp.concatenate(values, axis=0)
    high = values.astype(BF16)
    rest = (values - high.astype(F32)).astype(BF16)
    parts = jnp.concatenate([high, rest], axis=1)
    values_ref[...] = parts
    both = jnp.dot(same_ref[...], parts, preferred_element_type=F32)
    wide = both[:, :width] + both[:, width:]
    unit = slot_unit_ref[...]
    out = (wide - unit * jnp.sum(unit * wide, axis=-1, keepdims=True)) * slot_inv_ref[...]

    low = []
    for i in range(per_dev):
        wide_q = jnp.zeros((qtokens, width), F32)
        for c in range(per_dev):
            start = (c * per_dev + i) * qtokens
            wide_q += grads[i][c] * own_unit[start : start + qtokens]
            wide_q += grads[i][per_dev + c] * after_unit[start : start + qtokens]
        unit_i = q_unit[i * qtokens : (i + 1) * qtokens]
        out_q = (wide_q - unit_i * jnp.sum(unit_i * wide_q, axis=-1, keepdims=True)) * q_inv[
            i * qtokens : (i + 1) * qtokens
        ]
        out_q = jnp.where(split == 0, out_q[:tokens], out_q[tokens:])
        d_query_ref[i] = out_q
        low.append(out_q)
    low = jnp.concatenate([out] + low, axis=0).astype(BF16)
    low_ref[...] = low
    send_ref[...] = partial_sum(there_ref, low).astype(BF16)


def page_kernel(values_ref, low_ref, here_ref, table_ref, unit_ref, inv_ref, query_ref, out_hbm, d_query_hbm, keep_ref, out_ref, sem):
    width = unit_ref.shape[1]
    small = pltpu.make_async_copy(query_ref, d_query_hbm, sem.at[0])
    small.start()
    both = jnp.dot(table_ref[...], values_ref[...], preferred_element_type=F32)
    wide = both[:, :width] + both[:, width:]
    unit = unit_ref[...]
    out = (wide - unit * jnp.sum(unit * wide, axis=-1, keepdims=True)) * inv_ref[...]
    out_ref[...] = out.reshape(out_ref.shape)
    copy = pltpu.make_async_copy(out_ref, out_hbm, sem.at[1])
    copy.start()
    keep_ref[...] = partial_sum(here_ref, low_ref[...])
    small.wait()
    copy.wait()


def add_kernel(keep_ref, got_ref, out_ref):
    size = keep_ref.shape[0] // PLANES
    for z in range(PLANES):
        at = ((z & 1) * 4 + (z & 2) + (z >> 2)) * size
        here = slice(z * size, (z + 1) * size)
        out_ref[at : at + size] = (keep_ref[here] + got_ref[here].astype(F32)).astype(BF16)


def sum_kernel(parts_ref, out_ref):
    total = jnp.sum(parts_ref[...].astype(F32), axis=0)
    rows = out_ref.shape[0]
    out_ref[...] = total[:rows] + total[rows:]


def shards(page_hidden, query_hidden, page_pre, query_pre, match_index, positive):
    per_dev, patches_all, width = page_pre.shape
    qtokens = query_pre.shape[1]
    patches = page_hidden.shape[1]
    hidden = page_hidden.shape[2]
    groups = lax.axis_size(BLK)
    blocks = groups * 2
    pages = blocks * per_dev
    slots = per_dev * match_index.shape[1] * match_index.shape[2]
    page_t = jnp.transpose(page_pre, (1, 0, 2))
    hid_t = jnp.transpose(page_hidden, (1, 0, 2))
    limit = pltpu.CompilerParams(vmem_limit_bytes=24 * 2**20)
    place = pl.pallas_call(
        place_kernel,
        out_shape=jax.ShapeDtypeStruct((8, LANES), jnp.int32),
        out_specs=VMEM,
        compiler_params=limit,
        cost_estimate=pl.CostEstimate(flops=5 * 10**9, bytes_accessed=4096, transcendentals=0),
        name="place",
    )()
    count = slots // 2 + per_dev * qtokens + 16
    payload = jax.ShapeDtypeStruct((count, width), BF16)
    first, second, rows, half, misc = pl.pallas_call(
        functools.partial(gather_kernel, blocks),
        out_shape=(
            payload,
            payload,
            jax.ShapeDtypeStruct((slots, width), BF16),
            jax.ShapeDtypeStruct((patches, per_dev, width), BF16),
            jax.ShapeDtypeStruct((8, slots), jnp.int32),
        ),
        in_specs=[VMEM] * 5,
        out_specs=(VMEM,) * 5,
        compiler_params=limit,
        name="gather_rows",
    )(place, match_index, positive.reshape(1, per_dev), query_pre, page_t)
    swap = [(i, i ^ 1) for i in range(blocks)]
    cross = []
    for i in range(blocks):
        j = (i + 1) % blocks if i % 2 else (i - 1) % blocks
        for part in range(lax.axis_size("mp")):
            cross.append((2 * i + part, 2 * j + (part if i // (2 * RUN) == j // (2 * RUN) else 1 - part)))
    far = lax.ppermute(second, DP + ("mp",), cross)
    near = lax.ppermute(first, DP, swap)
    wide_rows = jax.ShapeDtypeStruct((patches * per_dev, width), F32)
    own_rows = jax.ShapeDtypeStruct((slots // 2, width), F32)
    own_queries = jax.ShapeDtypeStruct((per_dev * qtokens, width), F32)
    slot_rows = jax.ShapeDtypeStruct((slots, width), F32)
    share = hidden // (2 * groups)
    depth = slots + query_hidden.shape[0] * query_hidden.shape[1]
    by_core = jax.ShapeDtypeStruct((groups, share, depth), BF16)
    unit, inv, table, *local, here = pl.pallas_call(
        local_kernel,
        out_shape=(
            wide_rows,
            wide_rows,
            jax.ShapeDtypeStruct((patches * per_dev, slots), BF16),
            own_rows,
            own_rows,
            own_queries,
            own_queries,
            slot_rows,
            slot_rows,
            jax.ShapeDtypeStruct((slots, slots), BF16),
            by_core,
            by_core,
        ),
        in_specs=[VMEM] * 6,
        out_specs=(VMEM,) * 12,
        compiler_params=limit,
        cost_estimate=pl.CostEstimate(flops=5 * 10**9, bytes_accessed=10**6, transcendentals=0),
        name="local_rows",
    )(first, rows, half, misc, hid_t, query_hidden)
    d_query, values, low, send = pl.pallas_call(
        functools.partial(main_kernel, pages, per_dev),
        out_shape=(
            jax.ShapeDtypeStruct((per_dev, query_hidden.shape[1], width), F32),
            jax.ShapeDtypeStruct((slots, 2 * width), BF16),
            jax.ShapeDtypeStruct((depth, width), BF16),
            jax.ShapeDtypeStruct((groups, share, width), BF16),
        ),
        in_specs=[VMEM] * 11,
        out_specs=(VMEM,) * 4,
        compiler_params=limit,
        name="grads_and_partial",
    )(first, near, far, *local)
    got = lax.ppermute(send, "core", [(0, 1), (1, 0)])
    d_page, d_query, keep = pl.pallas_call(
        page_kernel,
        out_shape=(
            jax.ShapeDtypeStruct((patches, per_dev, width), F32),
            jax.ShapeDtypeStruct(d_query.shape, F32),
            jax.ShapeDtypeStruct((groups, share, width), F32),
        ),
        in_specs=[VMEM] * 7,
        out_specs=(ANY, ANY, VMEM),
        scratch_shapes=[pltpu.VMEM((patches, per_dev, width), F32), pltpu.SemaphoreType.DMA((2,))],
        compiler_params=limit,
        cost_estimate=pl.CostEstimate(flops=10**9, bytes_accessed=10**6, transcendentals=0),
        name="page_grads",
    )(values, low, here, table, unit, inv, d_query)
    small = pltpu.CompilerParams(vmem_limit_bytes=16 * 2**20)
    pair = pl.pallas_call(
        add_kernel,
        out_shape=jax.ShapeDtypeStruct(got.shape, BF16),
        in_specs=[VMEM, VMEM],
        out_specs=VMEM,
        compiler_params=small,
        name="add_pair",
    )(keep, got)
    parts = lax.all_to_all(pair.reshape(groups * 2, share // 2, width), ("z0", "z1", "z2", "run", "mp"), 0, 0, tiled=True)
    grad = pl.pallas_call(
        sum_kernel,
        out_shape=jax.ShapeDtypeStruct((share // 2, width), F32),
        in_specs=[VMEM],
        out_specs=VMEM,
        compiler_params=small,
        name="sum_parts",
    )(parts.reshape(groups, share, width))
    return jnp.transpose(d_page, (1, 0, 2)), d_query, grad


def solution(mesh):
    blocks, parts = mesh.devices.shape
    fine = Mesh(mesh.devices.reshape(2, 2, 2, blocks // 16, 2, parts), DP + ("mp",))
    placed = (
        P(DP, "mp", None),
        P(DP, "mp", None),
        P(DP, None, None),
        P(DP, None, None),
        P(DP, None, None),
        P(DP),
    )
    return jax.shard_map(
        shards,
        mesh=fine,
        in_specs=placed,
        out_specs=(P(DP, "mp", None), P(DP, "mp", None), P(DP + ("mp",), None)),
        check_vma=False,
    )
```

```python
import functools

import jax
import jax.numpy as jnp
from jax import lax
from jax.experimental import pallas as pl
from jax.experimental.pallas import tpu as pltpu
from jax.sharding import Mesh, PartitionSpec as P

SCALE_LOGIT = 10.0
EPS = 1e-06
F32 = jnp.float32
BF16 = jnp.bfloat16
LANES = 128
RUN = 4
PLANES = 8
BLK = ("z2", "z1", "z0", "run")
DP = BLK + ("core",)
RUNS = 8
ORDER = ("z0", "z1", "z2", "x0", "x1", "yh", "mp")
VMEM = pl.BlockSpec(memory_space=pltpu.VMEM)
ANY = pl.BlockSpec(memory_space=pl.ANY)


def exchange_order():
    names = ("z2", "z1", "z0", "yh", "x1", "x0", "core", "mp")
    members, places = ([], []), [0] * (PLANES * RUNS)
    for place in range(2 ** len(ORDER)):
        bits = {name: 1 - (place >> (len(ORDER) - 1 - i)) % 2 for i, name in enumerate(ORDER)}
        for core in range(2):
            bits["core"] = core
            device = functools.reduce(lambda total, name: total * 2 + bits[name], names, 0)
            members[core].append(device)
        places[device // 4] = place // 2
    return members, places


def one_hot(targets, rows):
    at = lax.broadcasted_iota(jnp.int16, (rows, targets.shape[1]), 0)
    return jnp.where(at == targets.astype(jnp.int16), jnp.ones((), BF16), jnp.zeros((), BF16))


def inverse_norm(wide):
    return lax.rsqrt(jnp.sum(wide * wide, axis=-1, keepdims=True) + EPS)


def rounded(wide):
    return wide.astype(BF16).astype(F32)


def rounded_unit(raw):
    wide = raw.astype(F32)
    return rounded(wide * inverse_norm(wide))


def place_kernel(out_ref):
    block = lax.axis_index(DP)
    out_ref[...] = jnp.full(out_ref.shape, block, jnp.int32)


def gather_kernel(blocks, place_ref, idx_ref, pos_ref, query_ref, page_ref, first_ref, second_ref, rows_ref, half_ref, misc_ref):
    patches, per_dev, width = page_ref.shape
    flat = patches * per_dev
    half = idx_ref.shape[2]
    spots = jnp.concatenate(
        [idx_ref[c, v : v + 1, :] * per_dev + c for c in range(per_dev) for v in range(idx_ref.shape[1])], axis=1
    )
    target = pos_ref[...]
    rows = lax.dot_general(
        one_hot(spots, flat),
        page_ref[...].reshape(flat, width),
        (((0,), (0,)), ((), ())),
        preferred_element_type=F32,
    ).astype(BF16)
    rows_ref[...] = rows
    own = jnp.concatenate([rows[2 * c * half : (2 * c + 1) * half] for c in range(per_dev)], axis=0)
    visiting = jnp.concatenate([rows[(2 * c + 1) * half : (2 * c + 2) * half] for c in range(per_dev)], axis=0)
    even = lax.axis_index("core") == 0
    shift = target // per_dev - place_ref[0:1, :per_dev] + blocks
    column = jnp.where(shift >= blocks, shift - blocks, shift) * per_dev + target % per_dev
    count = own.shape[0]
    first_ref[0:count, :] = jnp.where(even, own, visiting)
    second_ref[0:count, :] = jnp.where(even, visiting, own)
    lane = lax.broadcasted_iota(jnp.int32, (16, width), 1)
    meta = jnp.zeros((16, width), F32)
    for i in range(per_dev):
        meta = jnp.where(lane == i, column[:, i : i + 1].astype(F32), meta)
    tail = jnp.concatenate([query_ref[...].reshape(-1, width), meta.astype(BF16)], axis=0)
    first_ref[count:, :] = tail
    second_ref[count:, :] = tail
    half_rows = half_ref.shape[0]
    start = lax.axis_index("mp") * half_rows
    half_ref[...] = page_ref[pl.ds(start, half_rows)]
    misc_ref[...] = jnp.broadcast_to(spots - start * per_dev, misc_ref.shape)


def local_kernel(
    sent_ref, rows_ref, half_ref, misc_ref, hid_ref, qhid_ref, unit_ref, inv_ref, table_ref, own_ref, visit_ref, query_ref,
    qinv_ref, slot_unit_ref, slot_inv_ref, same_ref, there_ref, here_ref,
):
    patches, per_dev, width = half_ref.shape
    flat = patches * per_dev
    slots = rows_ref.shape[0]
    half = slots // (2 * per_dev)
    spots = misc_ref[0:1, :]
    table = one_hot(spots, flat)
    table_ref[...] = table
    page = half_ref[...].reshape(flat, width).astype(F32)
    inv = inverse_norm(page)
    unit_ref[...] = page * inv
    inv_ref[...] = jnp.broadcast_to(inv, (flat, width))
    wide = rows_ref[...].astype(F32)
    inv = inverse_norm(wide)
    slot_unit = wide * inv
    slot_unit_ref[...] = slot_unit
    for c in range(per_dev):
        own_ref[c * half : (c + 1) * half] = rounded(slot_unit[2 * c * half : (2 * c + 1) * half])
        visit_ref[c * half : (c + 1) * half] = rounded(slot_unit[(2 * c + 1) * half : (2 * c + 2) * half])
    column = misc_ref[...].astype(F32).T[:, 0:1]
    same = column == spots.astype(F32)
    earlier = lax.broadcasted_iota(jnp.int32, same.shape, 1) < lax.broadcasted_iota(jnp.int32, same.shape, 0)
    repeats = jnp.sum((same & earlier).astype(F32), axis=1, keepdims=True)
    counts = (repeats == 0) & (column >= 0) & (column < flat)
    same_ref[...] = same.astype(BF16)
    slot_inv_ref[...] = jnp.where(counts, inv, 0.0) + jnp.zeros((slots, width), F32)
    wide = sent_ref[per_dev * half : (per_dev + 1) * half, :].astype(F32)
    inv = inverse_norm(wide)
    query_ref[...] = wide * inv
    qinv_ref[...] = jnp.broadcast_to(inv, wide.shape)
    dims = (((0,), (0,)), ((), ()))
    tokens = qhid_ref.shape[0] * qhid_ref.shape[1]
    eye = one_hot(lax.broadcasted_iota(jnp.int32, (1, tokens), 1), tokens)
    picked = lax.dot_general(hid_ref[...].reshape(flat, -1), table, dims, preferred_element_type=F32)
    turned = lax.dot_general(qhid_ref[...].reshape(tokens, -1), eye, dims, preferred_element_type=F32)
    even = lax.axis_index("core") == 0
    groups, share, _ = here_ref.shape
    for part, at in ((picked, slice(0, slots)), (turned, slice(slots, slots + tokens))):
        part = part.astype(BF16).reshape(groups, 2, share, part.shape[1])
        here_ref[:, :, at] = jnp.where(even, part[:, 0], part[:, 1])
        there_ref[:, :, at] = jnp.where(even, part[:, 1], part[:, 0])


def loss_grads(unit_q, own_rows, other_rows, columns, per_dev, qtokens, pages):
    grads = []
    for i in range(per_dev):
        query = unit_q[i * qtokens : (i + 1) * qtokens]
        scores = []
        for rows in (own_rows, other_rows):
            for c in range(per_dev):
                start = (c * per_dev + i) * qtokens
                prods = jnp.sum(query * rows[start : start + qtokens], axis=0, keepdims=True)
                scores.append(SCALE_LOGIT * jnp.sum(prods, axis=1, keepdims=True))
        top = functools.reduce(jnp.maximum, scores)
        parts = [jnp.exp(s - top) for s in scores]
        total = functools.reduce(jnp.add, parts)
        grads.append(
            [
                (part / total - (columns[i] == j).astype(F32)) * (SCALE_LOGIT / pages)
                for j, part in enumerate(parts)
            ]
        )
    return grads


def partial_sum(hid_ref, low):
    groups, share, depth = hid_ref.shape
    total = jnp.dot(hid_ref[...].reshape(groups * share, depth), low, preferred_element_type=F32)
    return total.reshape(groups, share, low.shape[1])


def main_kernel(
    pages, per_dev, sent_ref, first_ref, second_ref, own_ref, visit_ref, query_ref, qinv_ref, slot_unit_ref,
    slot_inv_ref, same_ref, there_ref, d_query_ref, values_ref, low_ref, send_ref,
):
    qcount, width = query_ref.shape
    qtokens = qcount // per_dev
    tokens = d_query_ref.shape[1]
    split = lax.axis_index("mp")
    even = lax.axis_index("core") == 0
    count = own_ref.shape[0]

    first, second = first_ref[...], second_ref[...]
    after = jnp.where(even, first[:count], second[:count])
    before = jnp.where(even, second, first)
    own_unit = own_ref[...]
    visit_unit = visit_ref[...]
    after_unit = rounded_unit(after)
    before_rows = rounded_unit(before[:count])
    before_q = rounded_unit(before[count : count + qcount])
    q_unit = query_ref[...]
    q_inv = qinv_ref[...]
    q_low = q_unit.astype(BF16).astype(F32)

    own_meta = sent_ref[count + qcount :, :].astype(F32)
    before_meta = before[count + qcount :].astype(F32)
    columns = [own_meta[0:1, i : i + 1] for i in range(per_dev)]
    before_columns = [before_meta[0:1, i : i + 1] for i in range(per_dev)]
    grads = loss_grads(q_low, own_unit, after_unit, columns, per_dev, qtokens, pages)
    before_grads = loss_grads(before_q, before_rows, visit_unit, before_columns, per_dev, qtokens, pages)

    values = []
    for c in range(per_dev):
        for i in range(per_dev):
            values.append(grads[i][c] * q_low[i * qtokens : (i + 1) * qtokens])
        for i in range(per_dev):
            values.append(before_grads[i][per_dev + c] * before_q[i * qtokens : (i + 1) * qtokens])
    values = jnp.concatenate(values, axis=0)
    high = values.astype(BF16)
    rest = (values - high.astype(F32)).astype(BF16)
    parts = jnp.concatenate([high, rest], axis=1)
    values_ref[...] = parts
    both = jnp.dot(same_ref[...], parts, preferred_element_type=F32)
    wide = both[:, :width] + both[:, width:]
    unit = slot_unit_ref[...]
    out = (wide - unit * jnp.sum(unit * wide, axis=-1, keepdims=True)) * slot_inv_ref[...]

    low = []
    for i in range(per_dev):
        wide_q = jnp.zeros((qtokens, width), F32)
        for c in range(per_dev):
            start = (c * per_dev + i) * qtokens
            wide_q += grads[i][c] * own_unit[start : start + qtokens]
            wide_q += grads[i][per_dev + c] * after_unit[start : start + qtokens]
        unit_i = q_unit[i * qtokens : (i + 1) * qtokens]
        out_q = (wide_q - unit_i * jnp.sum(unit_i * wide_q, axis=-1, keepdims=True)) * q_inv[
            i * qtokens : (i + 1) * qtokens
        ]
        out_q = jnp.where(split == 0, out_q[:tokens], out_q[tokens:])
        d_query_ref[i] = out_q
        low.append(out_q)
    low = jnp.concatenate([out] + low, axis=0).astype(BF16)
    low_ref[...] = low
    send_ref[...] = partial_sum(there_ref, low).astype(BF16)


def page_kernel(values_ref, low_ref, here_ref, table_ref, unit_ref, inv_ref, query_ref, out_hbm, d_query_hbm, keep_ref, out_ref, sem):
    width = unit_ref.shape[1]
    small = pltpu.make_async_copy(query_ref, d_query_hbm, sem.at[0])
    small.start()
    both = jnp.dot(table_ref[...], values_ref[...], preferred_element_type=F32)
    wide = both[:, :width] + both[:, width:]
    unit = unit_ref[...]
    out = (wide - unit * jnp.sum(unit * wide, axis=-1, keepdims=True)) * inv_ref[...]
    out_ref[...] = out.reshape(out_ref.shape)
    copy = pltpu.make_async_copy(out_ref, out_hbm, sem.at[1])
    copy.start()
    keep_ref[...] = partial_sum(here_ref, low_ref[...])
    small.wait()
    copy.wait()


def add_kernel(keep_ref, got_ref, out_ref):
    rows = keep_ref.shape[1] // 2
    for group, place in enumerate(exchange_order()[1]):
        total = keep_ref[group] + got_ref[group].astype(F32)
        out_ref[place] = jnp.concatenate([total[rows:], total[:rows]], axis=0).astype(BF16)


def sum_kernel(parts_ref, out_ref):
    total = jnp.sum(parts_ref[...].astype(F32), axis=0)
    rows = out_ref.shape[0]
    out_ref[...] = total[:rows] + total[rows:]


def shards(page_hidden, query_hidden, page_pre, query_pre, match_index, positive):
    per_dev, patches_all, width = page_pre.shape
    qtokens = query_pre.shape[1]
    patches = page_hidden.shape[1]
    hidden = page_hidden.shape[2]
    groups = lax.axis_size(BLK)
    blocks = groups * 2
    pages = blocks * per_dev
    slots = per_dev * match_index.shape[1] * match_index.shape[2]
    page_t = jnp.transpose(page_pre, (1, 0, 2))
    hid_t = jnp.transpose(page_hidden, (1, 0, 2))
    limit = pltpu.CompilerParams(vmem_limit_bytes=24 * 2**20)
    place = pl.pallas_call(
        place_kernel,
        out_shape=jax.ShapeDtypeStruct((8, LANES), jnp.int32),
        out_specs=VMEM,
        compiler_params=limit,
        cost_estimate=pl.CostEstimate(flops=5 * 10**9, bytes_accessed=4096, transcendentals=0),
        name="place",
    )()
    count = slots // 2 + per_dev * qtokens + 16
    payload = jax.ShapeDtypeStruct((count, width), BF16)
    first, second, rows, half, misc = pl.pallas_call(
        functools.partial(gather_kernel, blocks),
        out_shape=(
            payload,
            payload,
            jax.ShapeDtypeStruct((slots, width), BF16),
            jax.ShapeDtypeStruct((patches, per_dev, width), BF16),
            jax.ShapeDtypeStruct((8, slots), jnp.int32),
        ),
        in_specs=[VMEM] * 5,
        out_specs=(VMEM,) * 5,
        compiler_params=limit,
        name="gather_rows",
    )(place, match_index, positive.reshape(1, per_dev), query_pre, page_t)
    swap = [(i, i ^ 1) for i in range(blocks)]
    cross = []
    for i in range(blocks):
        j = (i + 1) % blocks if i % 2 else (i - 1) % blocks
        for part in range(lax.axis_size("mp")):
            cross.append((2 * i + part, 2 * j + (part if i // (2 * RUN) == j // (2 * RUN) else 1 - part)))
    far = lax.ppermute(second, DP + ("mp",), cross)
    near = lax.ppermute(first, DP, swap)
    wide_rows = jax.ShapeDtypeStruct((patches * per_dev, width), F32)
    own_rows = jax.ShapeDtypeStruct((slots // 2, width), F32)
    own_queries = jax.ShapeDtypeStruct((per_dev * qtokens, width), F32)
    slot_rows = jax.ShapeDtypeStruct((slots, width), F32)
    share = hidden // (2 * groups)
    depth = slots + query_hidden.shape[0] * query_hidden.shape[1]
    by_core = jax.ShapeDtypeStruct((groups, share, depth), BF16)
    unit, inv, table, *local, here = pl.pallas_call(
        local_kernel,
        out_shape=(
            wide_rows,
            wide_rows,
            jax.ShapeDtypeStruct((patches * per_dev, slots), BF16),
            own_rows,
            own_rows,
            own_queries,
            own_queries,
            slot_rows,
            slot_rows,
            jax.ShapeDtypeStruct((slots, slots), BF16),
            by_core,
            by_core,
        ),
        in_specs=[VMEM] * 6,
        out_specs=(VMEM,) * 12,
        compiler_params=limit,
        cost_estimate=pl.CostEstimate(flops=5 * 10**9, bytes_accessed=10**6, transcendentals=0),
        name="local_rows",
    )(first, rows, half, misc, hid_t, query_hidden)
    d_query, values, low, send = pl.pallas_call(
        functools.partial(main_kernel, pages, per_dev),
        out_shape=(
            jax.ShapeDtypeStruct((per_dev, query_hidden.shape[1], width), F32),
            jax.ShapeDtypeStruct((slots, 2 * width), BF16),
            jax.ShapeDtypeStruct((depth, width), BF16),
            jax.ShapeDtypeStruct((groups, share, width), BF16),
        ),
        in_specs=[VMEM] * 11,
        out_specs=(VMEM,) * 4,
        compiler_params=limit,
        name="grads_and_partial",
    )(first, near, far, *local)
    got = lax.ppermute(send, "core", [(0, 1), (1, 0)])
    d_page, d_query, keep = pl.pallas_call(
        page_kernel,
        out_shape=(
            jax.ShapeDtypeStruct((patches, per_dev, width), F32),
            jax.ShapeDtypeStruct(d_query.shape, F32),
            jax.ShapeDtypeStruct((groups, share, width), F32),
        ),
        in_specs=[VMEM] * 7,
        out_specs=(ANY, ANY, VMEM),
        scratch_shapes=[pltpu.VMEM((patches, per_dev, width), F32), pltpu.SemaphoreType.DMA((2,))],
        compiler_params=limit,
        cost_estimate=pl.CostEstimate(flops=10**9, bytes_accessed=10**6, transcendentals=0),
        name="page_grads",
    )(values, low, here, table, unit, inv, d_query)
    small = pltpu.CompilerParams(vmem_limit_bytes=16 * 2**20)
    pair = pl.pallas_call(
        add_kernel,
        out_shape=jax.ShapeDtypeStruct(got.shape, BF16),
        in_specs=[VMEM, VMEM],
        out_specs=VMEM,
        compiler_params=small,
        name="add_pair",
    )(keep, got)
    parts = lax.all_to_all(
        pair.reshape(groups * 2, share // 2, width),
        DP + ("mp",),
        0,
        0,
        tiled=True,
        axis_index_groups=exchange_order()[0],
    )
    grad = pl.pallas_call(
        sum_kernel,
        out_shape=jax.ShapeDtypeStruct((share // 2, width), F32),
        in_specs=[VMEM],
        out_specs=VMEM,
        compiler_params=small,
        name="sum_parts",
    )(parts.reshape(groups, share, width))
    return jnp.transpose(d_page, (1, 0, 2)), d_query, grad


def solution(mesh):
    blocks, parts = mesh.devices.shape
    fine = Mesh(mesh.devices.reshape(2, 2, 2, blocks // 16, 2, parts), DP + ("mp",))
    placed = (
        P(DP, "mp", None),
        P(DP, "mp", None),
        P(DP, None, None),
        P(DP, None, None),
        P(DP, None, None),
        P(DP),
    )
    return jax.shard_map(
        shards,
        mesh=fine,
        in_specs=placed,
        out_specs=(P(DP, "mp", None), P(DP, "mp", None), P(DP + ("mp",), None)),
        check_vma=False,
    )
```

```python
import functools

import jax
import jax.numpy as jnp
from jax import lax
from jax.experimental import pallas as pl
from jax.experimental.pallas import tpu as pltpu
from jax.sharding import Mesh, PartitionSpec as P

SCALE_LOGIT = 10.0
EPS = 1e-06
F32 = jnp.float32
BF16 = jnp.bfloat16
LANES = 128
RUN = 4
PLANES = 8
BLK = ("z2", "z1", "z0", "run")
DP = BLK + ("core",)
RUNS = 8
ORDER = ("z0", "z1", "z2", "x0", "x1", "yh", "mp")
VMEM = pl.BlockSpec(memory_space=pltpu.VMEM)
ANY = pl.BlockSpec(memory_space=pl.ANY)


def exchange_order():
    names = ("z2", "z1", "z0", "yh", "x1", "x0", "core", "mp")
    members, places = ([], []), [0] * (PLANES * RUNS)
    for place in range(2 ** len(ORDER)):
        bits = {name: (place >> (len(ORDER) - 1 - i)) % 2 for i, name in enumerate(ORDER)}
        bits = {name: bit if name == "mp" else 1 - bit for name, bit in bits.items()}
        for core in range(2):
            bits["core"] = core
            device = functools.reduce(lambda total, name: total * 2 + bits[name], names, 0)
            members[core].append(device)
        places[device // 4] = place // 2
    return members, places


def one_hot(targets, rows):
    at = lax.broadcasted_iota(jnp.int16, (rows, targets.shape[1]), 0)
    return jnp.where(at == targets.astype(jnp.int16), jnp.ones((), BF16), jnp.zeros((), BF16))


def inverse_norm(wide):
    return lax.rsqrt(jnp.sum(wide * wide, axis=-1, keepdims=True) + EPS)


def rounded(wide):
    return wide.astype(BF16).astype(F32)


def rounded_unit(raw):
    wide = raw.astype(F32)
    return rounded(wide * inverse_norm(wide))


def place_kernel(out_ref):
    block = lax.axis_index(DP)
    out_ref[...] = jnp.full(out_ref.shape, block, jnp.int32)


def gather_kernel(blocks, place_ref, idx_ref, pos_ref, query_ref, page_ref, first_ref, second_ref, rows_ref, half_ref, misc_ref):
    patches, per_dev, width = page_ref.shape
    flat = patches * per_dev
    half = idx_ref.shape[2]
    spots = jnp.concatenate(
        [idx_ref[c, v : v + 1, :] * per_dev + c for c in range(per_dev) for v in range(idx_ref.shape[1])], axis=1
    )
    target = pos_ref[...]
    rows = lax.dot_general(
        one_hot(spots, flat),
        page_ref[...].reshape(flat, width),
        (((0,), (0,)), ((), ())),
        preferred_element_type=F32,
    ).astype(BF16)
    rows_ref[...] = rows
    own = jnp.concatenate([rows[2 * c * half : (2 * c + 1) * half] for c in range(per_dev)], axis=0)
    visiting = jnp.concatenate([rows[(2 * c + 1) * half : (2 * c + 2) * half] for c in range(per_dev)], axis=0)
    even = lax.axis_index("core") == 0
    shift = target // per_dev - place_ref[0:1, :per_dev] + blocks
    column = jnp.where(shift >= blocks, shift - blocks, shift) * per_dev + target % per_dev
    count = own.shape[0]
    first_ref[0:count, :] = jnp.where(even, own, visiting)
    second_ref[0:count, :] = jnp.where(even, visiting, own)
    lane = lax.broadcasted_iota(jnp.int32, (16, width), 1)
    meta = jnp.zeros((16, width), F32)
    for i in range(per_dev):
        meta = jnp.where(lane == i, column[:, i : i + 1].astype(F32), meta)
    tail = jnp.concatenate([query_ref[...].reshape(-1, width), meta.astype(BF16)], axis=0)
    first_ref[count:, :] = tail
    second_ref[count:, :] = tail
    half_rows = half_ref.shape[0]
    start = lax.axis_index("mp") * half_rows
    half_ref[...] = page_ref[pl.ds(start, half_rows)]
    misc_ref[...] = jnp.broadcast_to(spots - start * per_dev, misc_ref.shape)


def local_kernel(
    sent_ref, rows_ref, half_ref, misc_ref, hid_ref, qhid_ref, unit_ref, inv_ref, table_ref, own_ref, visit_ref, query_ref,
    qinv_ref, slot_unit_ref, slot_inv_ref, same_ref, there_ref, here_ref,
):
    patches, per_dev, width = half_ref.shape
    flat = patches * per_dev
    slots = rows_ref.shape[0]
    half = slots // (2 * per_dev)
    spots = misc_ref[0:1, :]
    table = one_hot(spots, flat)
    table_ref[...] = table
    page = half_ref[...].reshape(flat, width).astype(F32)
    inv = inverse_norm(page)
    unit_ref[...] = page * inv
    inv_ref[...] = jnp.broadcast_to(inv, (flat, width))
    wide = rows_ref[...].astype(F32)
    inv = inverse_norm(wide)
    slot_unit = wide * inv
    slot_unit_ref[...] = slot_unit
    for c in range(per_dev):
        own_ref[c * half : (c + 1) * half] = rounded(slot_unit[2 * c * half : (2 * c + 1) * half])
        visit_ref[c * half : (c + 1) * half] = rounded(slot_unit[(2 * c + 1) * half : (2 * c + 2) * half])
    column = misc_ref[...].astype(F32).T[:, 0:1]
    same = column == spots.astype(F32)
    earlier = lax.broadcasted_iota(jnp.int32, same.shape, 1) < lax.broadcasted_iota(jnp.int32, same.shape, 0)
    repeats = jnp.sum((same & earlier).astype(F32), axis=1, keepdims=True)
    counts = (repeats == 0) & (column >= 0) & (column < flat)
    same_ref[...] = same.astype(BF16)
    slot_inv_ref[...] = jnp.where(counts, inv, 0.0) + jnp.zeros((slots, width), F32)
    wide = sent_ref[per_dev * half : (per_dev + 1) * half, :].astype(F32)
    inv = inverse_norm(wide)
    query_ref[...] = wide * inv
    qinv_ref[...] = jnp.broadcast_to(inv, wide.shape)
    dims = (((0,), (0,)), ((), ()))
    tokens = qhid_ref.shape[0] * qhid_ref.shape[1]
    eye = one_hot(lax.broadcasted_iota(jnp.int32, (1, tokens), 1), tokens)
    picked = lax.dot_general(hid_ref[...].reshape(flat, -1), table, dims, preferred_element_type=F32)
    turned = lax.dot_general(qhid_ref[...].reshape(tokens, -1), eye, dims, preferred_element_type=F32)
    even = lax.axis_index("core") == 0
    groups, share, _ = here_ref.shape
    for part, at in ((picked, slice(0, slots)), (turned, slice(slots, slots + tokens))):
        part = part.astype(BF16).reshape(groups, 2, share, part.shape[1])
        here_ref[:, :, at] = jnp.where(even, part[:, 0], part[:, 1])
        there_ref[:, :, at] = jnp.where(even, part[:, 1], part[:, 0])


def loss_grads(unit_q, own_rows, other_rows, columns, per_dev, qtokens, pages):
    grads = []
    for i in range(per_dev):
        query = unit_q[i * qtokens : (i + 1) * qtokens]
        scores = []
        for rows in (own_rows, other_rows):
            for c in range(per_dev):
                start = (c * per_dev + i) * qtokens
                prods = jnp.sum(query * rows[start : start + qtokens], axis=0, keepdims=True)
                scores.append(SCALE_LOGIT * jnp.sum(prods, axis=1, keepdims=True))
        top = functools.reduce(jnp.maximum, scores)
        parts = [jnp.exp(s - top) for s in scores]
        total = functools.reduce(jnp.add, parts)
        grads.append(
            [
                (part / total - (columns[i] == j).astype(F32)) * (SCALE_LOGIT / pages)
                for j, part in enumerate(parts)
            ]
        )
    return grads


def partial_sum(hid_ref, low):
    groups, share, depth = hid_ref.shape
    total = jnp.dot(hid_ref[...].reshape(groups * share, depth), low, preferred_element_type=F32)
    return total.reshape(groups, share, low.shape[1])


def main_kernel(
    pages, per_dev, sent_ref, first_ref, second_ref, own_ref, visit_ref, query_ref, qinv_ref, slot_unit_ref,
    slot_inv_ref, same_ref, there_ref, d_query_ref, values_ref, low_ref, send_ref,
):
    qcount, width = query_ref.shape
    qtokens = qcount // per_dev
    tokens = d_query_ref.shape[1]
    split = lax.axis_index("mp")
    even = lax.axis_index("core") == 0
    count = own_ref.shape[0]

    first, second = first_ref[...], second_ref[...]
    after = jnp.where(even, first[:count], second[:count])
    before = jnp.where(even, second, first)
    own_unit = own_ref[...]
    visit_unit = visit_ref[...]
    after_unit = rounded_unit(after)
    before_rows = rounded_unit(before[:count])
    before_q = rounded_unit(before[count : count + qcount])
    q_unit = query_ref[...]
    q_inv = qinv_ref[...]
    q_low = q_unit.astype(BF16).astype(F32)

    own_meta = sent_ref[count + qcount :, :].astype(F32)
    before_meta = before[count + qcount :].astype(F32)
    columns = [own_meta[0:1, i : i + 1] for i in range(per_dev)]
    before_columns = [before_meta[0:1, i : i + 1] for i in range(per_dev)]
    grads = loss_grads(q_low, own_unit, after_unit, columns, per_dev, qtokens, pages)
    before_grads = loss_grads(before_q, before_rows, visit_unit, before_columns, per_dev, qtokens, pages)

    values = []
    for c in range(per_dev):
        for i in range(per_dev):
            values.append(grads[i][c] * q_low[i * qtokens : (i + 1) * qtokens])
        for i in range(per_dev):
            values.append(before_grads[i][per_dev + c] * before_q[i * qtokens : (i + 1) * qtokens])
    values = jnp.concatenate(values, axis=0)
    high = values.astype(BF16)
    rest = (values - high.astype(F32)).astype(BF16)
    parts = jnp.concatenate([high, rest], axis=1)
    values_ref[...] = parts
    both = jnp.dot(same_ref[...], parts, preferred_element_type=F32)
    wide = both[:, :width] + both[:, width:]
    unit = slot_unit_ref[...]
    out = (wide - unit * jnp.sum(unit * wide, axis=-1, keepdims=True)) * slot_inv_ref[...]

    low = []
    for i in range(per_dev):
        wide_q = jnp.zeros((qtokens, width), F32)
        for c in range(per_dev):
            start = (c * per_dev + i) * qtokens
            wide_q += grads[i][c] * own_unit[start : start + qtokens]
            wide_q += grads[i][per_dev + c] * after_unit[start : start + qtokens]
        unit_i = q_unit[i * qtokens : (i + 1) * qtokens]
        out_q = (wide_q - unit_i * jnp.sum(unit_i * wide_q, axis=-1, keepdims=True)) * q_inv[
            i * qtokens : (i + 1) * qtokens
        ]
        out_q = jnp.where(split == 0, out_q[:tokens], out_q[tokens:])
        d_query_ref[i] = out_q
        low.append(out_q)
    low = jnp.concatenate([out] + low, axis=0).astype(BF16)
    low_ref[...] = low
    send_ref[...] = partial_sum(there_ref, low).astype(BF16)


def page_kernel(values_ref, low_ref, here_ref, table_ref, unit_ref, inv_ref, query_ref, out_hbm, d_query_hbm, keep_ref, out_ref, sem):
    width = unit_ref.shape[1]
    small = pltpu.make_async_copy(query_ref, d_query_hbm, sem.at[0])
    small.start()
    both = jnp.dot(table_ref[...], values_ref[...], preferred_element_type=F32)
    wide = both[:, :width] + both[:, width:]
    unit = unit_ref[...]
    out = (wide - unit * jnp.sum(unit * wide, axis=-1, keepdims=True)) * inv_ref[...]
    out_ref[...] = out.reshape(out_ref.shape)
    copy = pltpu.make_async_copy(out_ref, out_hbm, sem.at[1])
    copy.start()
    keep_ref[...] = partial_sum(here_ref, low_ref[...])
    small.wait()
    copy.wait()


def add_kernel(keep_ref, got_ref, out_ref):
    for group, place in enumerate(exchange_order()[1]):
        out_ref[place] = (keep_ref[group] + got_ref[group].astype(F32)).astype(BF16)


def sum_kernel(parts_ref, out_ref):
    total = jnp.sum(parts_ref[...].astype(F32), axis=0)
    rows = out_ref.shape[0]
    out_ref[...] = total[:rows] + total[rows:]


def shards(page_hidden, query_hidden, page_pre, query_pre, match_index, positive):
    per_dev, patches_all, width = page_pre.shape
    qtokens = query_pre.shape[1]
    patches = page_hidden.shape[1]
    hidden = page_hidden.shape[2]
    groups = lax.axis_size(BLK)
    blocks = groups * 2
    pages = blocks * per_dev
    slots = per_dev * match_index.shape[1] * match_index.shape[2]
    page_t = jnp.transpose(page_pre, (1, 0, 2))
    hid_t = jnp.transpose(page_hidden, (1, 0, 2))
    limit = pltpu.CompilerParams(vmem_limit_bytes=24 * 2**20)
    place = pl.pallas_call(
        place_kernel,
        out_shape=jax.ShapeDtypeStruct((8, LANES), jnp.int32),
        out_specs=VMEM,
        compiler_params=limit,
        cost_estimate=pl.CostEstimate(flops=5 * 10**9, bytes_accessed=4096, transcendentals=0),
        name="place",
    )()
    count = slots // 2 + per_dev * qtokens + 16
    payload = jax.ShapeDtypeStruct((count, width), BF16)
    first, second, rows, half, misc = pl.pallas_call(
        functools.partial(gather_kernel, blocks),
        out_shape=(
            payload,
            payload,
            jax.ShapeDtypeStruct((slots, width), BF16),
            jax.ShapeDtypeStruct((patches, per_dev, width), BF16),
            jax.ShapeDtypeStruct((8, slots), jnp.int32),
        ),
        in_specs=[VMEM] * 5,
        out_specs=(VMEM,) * 5,
        compiler_params=limit,
        name="gather_rows",
    )(place, match_index, positive.reshape(1, per_dev), query_pre, page_t)
    swap = [(i, i ^ 1) for i in range(blocks)]
    cross = []
    for i in range(blocks):
        j = (i + 1) % blocks if i % 2 else (i - 1) % blocks
        for part in range(lax.axis_size("mp")):
            cross.append((2 * i + part, 2 * j + (part if i // (2 * RUN) == j // (2 * RUN) else 1 - part)))
    far = lax.ppermute(second, DP + ("mp",), cross)
    near = lax.ppermute(first, DP, swap)
    wide_rows = jax.ShapeDtypeStruct((patches * per_dev, width), F32)
    own_rows = jax.ShapeDtypeStruct((slots // 2, width), F32)
    own_queries = jax.ShapeDtypeStruct((per_dev * qtokens, width), F32)
    slot_rows = jax.ShapeDtypeStruct((slots, width), F32)
    share = hidden // (2 * groups)
    depth = slots + query_hidden.shape[0] * query_hidden.shape[1]
    by_core = jax.ShapeDtypeStruct((groups, share, depth), BF16)
    unit, inv, table, *local, here = pl.pallas_call(
        local_kernel,
        out_shape=(
            wide_rows,
            wide_rows,
            jax.ShapeDtypeStruct((patches * per_dev, slots), BF16),
            own_rows,
            own_rows,
            own_queries,
            own_queries,
            slot_rows,
            slot_rows,
            jax.ShapeDtypeStruct((slots, slots), BF16),
            by_core,
            by_core,
        ),
        in_specs=[VMEM] * 6,
        out_specs=(VMEM,) * 12,
        compiler_params=limit,
        cost_estimate=pl.CostEstimate(flops=5 * 10**9, bytes_accessed=10**6, transcendentals=0),
        name="local_rows",
    )(first, rows, half, misc, hid_t, query_hidden)
    d_query, values, low, send = pl.pallas_call(
        functools.partial(main_kernel, pages, per_dev),
        out_shape=(
            jax.ShapeDtypeStruct((per_dev, query_hidden.shape[1], width), F32),
            jax.ShapeDtypeStruct((slots, 2 * width), BF16),
            jax.ShapeDtypeStruct((depth, width), BF16),
            jax.ShapeDtypeStruct((groups, share, width), BF16),
        ),
        in_specs=[VMEM] * 11,
        out_specs=(VMEM,) * 4,
        compiler_params=limit,
        name="grads_and_partial",
    )(first, near, far, *local)
    got = lax.ppermute(send, "core", [(0, 1), (1, 0)])
    d_page, d_query, keep = pl.pallas_call(
        page_kernel,
        out_shape=(
            jax.ShapeDtypeStruct((patches, per_dev, width), F32),
            jax.ShapeDtypeStruct(d_query.shape, F32),
            jax.ShapeDtypeStruct((groups, share, width), F32),
        ),
        in_specs=[VMEM] * 7,
        out_specs=(ANY, ANY, VMEM),
        scratch_shapes=[pltpu.VMEM((patches, per_dev, width), F32), pltpu.SemaphoreType.DMA((2,))],
        compiler_params=limit,
        cost_estimate=pl.CostEstimate(flops=10**9, bytes_accessed=10**6, transcendentals=0),
        name="page_grads",
    )(values, low, here, table, unit, inv, d_query)
    small = pltpu.CompilerParams(vmem_limit_bytes=16 * 2**20)
    pair = pl.pallas_call(
        add_kernel,
        out_shape=jax.ShapeDtypeStruct(got.shape, BF16),
        in_specs=[VMEM, VMEM],
        out_specs=VMEM,
        compiler_params=small,
        name="add_pair",
    )(keep, got)
    parts = lax.all_to_all(
        pair.reshape(groups * 2, share // 2, width),
        DP + ("mp",),
        0,
        0,
        tiled=True,
        axis_index_groups=exchange_order()[0],
    )
    grad = pl.pallas_call(
        sum_kernel,
        out_shape=jax.ShapeDtypeStruct((share // 2, width), F32),
        in_specs=[VMEM],
        out_specs=VMEM,
        compiler_params=small,
        name="sum_parts",
    )(parts.reshape(groups, share, width))
    return jnp.transpose(d_page, (1, 0, 2)), d_query, grad


def solution(mesh):
    blocks, parts = mesh.devices.shape
    fine = Mesh(mesh.devices.reshape(2, 2, 2, blocks // 16, 2, parts), DP + ("mp",))
    placed = (
        P(DP, "mp", None),
        P(DP, "mp", None),
        P(DP, None, None),
        P(DP, None, None),
        P(DP, None, None),
        P(DP),
    )
    return jax.shard_map(
        shards,
        mesh=fine,
        in_specs=placed,
        out_specs=(P(DP, "mp", None), P(DP, "mp", None), P(DP + ("mp",), None)),
        check_vma=False,
    )
```

```python
import functools

import jax
import jax.numpy as jnp
from jax import lax
from jax.experimental import pallas as pl
from jax.experimental.pallas import tpu as pltpu
from jax.sharding import Mesh, PartitionSpec as P

SCALE_LOGIT = 10.0
EPS = 1e-06
F32 = jnp.float32
BF16 = jnp.bfloat16
LANES = 128
RUN = 4
PLANES = 8
BLK = ("z2", "z1", "z0", "run")
DP = BLK + ("core",)
RUNS = 8
ORDERS = (("z0", "z1", "z2", "x0", "x1", "yh", "mp"), ("z0", "z1", "z2", "yh", "x1", "x0", "mp"))
VMEM = pl.BlockSpec(memory_space=pltpu.VMEM)
ANY = pl.BlockSpec(memory_space=pl.ANY)


def exchange_order():
    names = ("z2", "z1", "z0", "yh", "x1", "x0", "core", "mp")
    members, places = ([], []), ([0] * (PLANES * RUNS), [0] * (PLANES * RUNS))
    for core, order in enumerate(ORDERS):
        for place in range(2 ** len(order)):
            bits = {name: (place >> (len(order) - 1 - i)) % 2 for i, name in enumerate(order)}
            bits = {name: bit if name == "mp" else 1 - bit for name, bit in bits.items()}
            bits["core"] = core
            device = functools.reduce(lambda total, name: total * 2 + bits[name], names, 0)
            members[core].append(device)
            places[core][device // 4] = place // 2
    return members, places


def one_hot(targets, rows):
    at = lax.broadcasted_iota(jnp.int16, (rows, targets.shape[1]), 0)
    return jnp.where(at == targets.astype(jnp.int16), jnp.ones((), BF16), jnp.zeros((), BF16))


def inverse_norm(wide):
    return lax.rsqrt(jnp.sum(wide * wide, axis=-1, keepdims=True) + EPS)


def rounded(wide):
    return wide.astype(BF16).astype(F32)


def rounded_unit(raw):
    wide = raw.astype(F32)
    return rounded(wide * inverse_norm(wide))


def place_kernel(out_ref):
    block = lax.axis_index(DP)
    out_ref[...] = jnp.full(out_ref.shape, block, jnp.int32)


def gather_kernel(blocks, place_ref, idx_ref, pos_ref, query_ref, page_ref, first_ref, second_ref, rows_ref, half_ref, misc_ref):
    patches, per_dev, width = page_ref.shape
    flat = patches * per_dev
    half = idx_ref.shape[2]
    spots = jnp.concatenate(
        [idx_ref[c, v : v + 1, :] * per_dev + c for c in range(per_dev) for v in range(idx_ref.shape[1])], axis=1
    )
    target = pos_ref[...]
    rows = lax.dot_general(
        one_hot(spots, flat),
        page_ref[...].reshape(flat, width),
        (((0,), (0,)), ((), ())),
        preferred_element_type=F32,
    ).astype(BF16)
    rows_ref[...] = rows
    own = jnp.concatenate([rows[2 * c * half : (2 * c + 1) * half] for c in range(per_dev)], axis=0)
    visiting = jnp.concatenate([rows[(2 * c + 1) * half : (2 * c + 2) * half] for c in range(per_dev)], axis=0)
    even = lax.axis_index("core") == 0
    shift = target // per_dev - place_ref[0:1, :per_dev] + blocks
    column = jnp.where(shift >= blocks, shift - blocks, shift) * per_dev + target % per_dev
    count = own.shape[0]
    first_ref[0:count, :] = jnp.where(even, own, visiting)
    second_ref[0:count, :] = jnp.where(even, visiting, own)
    lane = lax.broadcasted_iota(jnp.int32, (16, width), 1)
    meta = jnp.zeros((16, width), F32)
    for i in range(per_dev):
        meta = jnp.where(lane == i, column[:, i : i + 1].astype(F32), meta)
    tail = jnp.concatenate([query_ref[...].reshape(-1, width), meta.astype(BF16)], axis=0)
    first_ref[count:, :] = tail
    second_ref[count:, :] = tail
    half_rows = half_ref.shape[0]
    start = lax.axis_index("mp") * half_rows
    half_ref[...] = page_ref[pl.ds(start, half_rows)]
    misc_ref[...] = jnp.broadcast_to(spots - start * per_dev, misc_ref.shape)


def local_kernel(
    sent_ref, rows_ref, half_ref, misc_ref, hid_ref, qhid_ref, unit_ref, inv_ref, table_ref, own_ref, visit_ref, query_ref,
    qinv_ref, slot_unit_ref, slot_inv_ref, same_ref, there_ref, here_ref,
):
    patches, per_dev, width = half_ref.shape
    flat = patches * per_dev
    slots = rows_ref.shape[0]
    half = slots // (2 * per_dev)
    spots = misc_ref[0:1, :]
    table = one_hot(spots, flat)
    table_ref[...] = table
    page = half_ref[...].reshape(flat, width).astype(F32)
    inv = inverse_norm(page)
    unit_ref[...] = page * inv
    inv_ref[...] = jnp.broadcast_to(inv, (flat, width))
    wide = rows_ref[...].astype(F32)
    inv = inverse_norm(wide)
    slot_unit = wide * inv
    slot_unit_ref[...] = slot_unit
    for c in range(per_dev):
        own_ref[c * half : (c + 1) * half] = rounded(slot_unit[2 * c * half : (2 * c + 1) * half])
        visit_ref[c * half : (c + 1) * half] = rounded(slot_unit[(2 * c + 1) * half : (2 * c + 2) * half])
    column = misc_ref[...].astype(F32).T[:, 0:1]
    same = column == spots.astype(F32)
    earlier = lax.broadcasted_iota(jnp.int32, same.shape, 1) < lax.broadcasted_iota(jnp.int32, same.shape, 0)
    repeats = jnp.sum((same & earlier).astype(F32), axis=1, keepdims=True)
    counts = (repeats == 0) & (column >= 0) & (column < flat)
    same_ref[...] = same.astype(BF16)
    slot_inv_ref[...] = jnp.where(counts, inv, 0.0) + jnp.zeros((slots, width), F32)
    wide = sent_ref[per_dev * half : (per_dev + 1) * half, :].astype(F32)
    inv = inverse_norm(wide)
    query_ref[...] = wide * inv
    qinv_ref[...] = jnp.broadcast_to(inv, wide.shape)
    dims = (((0,), (0,)), ((), ()))
    tokens = qhid_ref.shape[0] * qhid_ref.shape[1]
    eye = one_hot(lax.broadcasted_iota(jnp.int32, (1, tokens), 1), tokens)
    picked = lax.dot_general(hid_ref[...].reshape(flat, -1), table, dims, preferred_element_type=F32)
    turned = lax.dot_general(qhid_ref[...].reshape(tokens, -1), eye, dims, preferred_element_type=F32)
    even = lax.axis_index("core") == 0
    groups, share, _ = here_ref.shape
    for part, at in ((picked, slice(0, slots)), (turned, slice(slots, slots + tokens))):
        part = part.astype(BF16).reshape(groups, 2, share, part.shape[1])
        here_ref[:, :, at] = jnp.where(even, part[:, 0], part[:, 1])
        there_ref[:, :, at] = jnp.where(even, part[:, 1], part[:, 0])


def loss_grads(unit_q, own_rows, other_rows, columns, per_dev, qtokens, pages):
    grads = []
    for i in range(per_dev):
        query = unit_q[i * qtokens : (i + 1) * qtokens]
        scores = []
        for rows in (own_rows, other_rows):
            for c in range(per_dev):
                start = (c * per_dev + i) * qtokens
                prods = jnp.sum(query * rows[start : start + qtokens], axis=0, keepdims=True)
                scores.append(SCALE_LOGIT * jnp.sum(prods, axis=1, keepdims=True))
        top = functools.reduce(jnp.maximum, scores)
        parts = [jnp.exp(s - top) for s in scores]
        total = functools.reduce(jnp.add, parts)
        grads.append(
            [
                (part / total - (columns[i] == j).astype(F32)) * (SCALE_LOGIT / pages)
                for j, part in enumerate(parts)
            ]
        )
    return grads


def partial_sum(hid_ref, low):
    groups, share, depth = hid_ref.shape
    total = jnp.dot(hid_ref[...].reshape(groups * share, depth), low, preferred_element_type=F32)
    return total.reshape(groups, share, low.shape[1])


def main_kernel(
    pages, per_dev, sent_ref, first_ref, second_ref, own_ref, visit_ref, query_ref, qinv_ref, slot_unit_ref,
    slot_inv_ref, same_ref, there_ref, d_query_ref, values_ref, low_ref, send_ref,
):
    qcount, width = query_ref.shape
    qtokens = qcount // per_dev
    tokens = d_query_ref.shape[1]
    split = lax.axis_index("mp")
    even = lax.axis_index("core") == 0
    count = own_ref.shape[0]

    first, second = first_ref[...], second_ref[...]
    after = jnp.where(even, first[:count], second[:count])
    before = jnp.where(even, second, first)
    own_unit = own_ref[...]
    visit_unit = visit_ref[...]
    after_unit = rounded_unit(after)
    before_rows = rounded_unit(before[:count])
    before_q = rounded_unit(before[count : count + qcount])
    q_unit = query_ref[...]
    q_inv = qinv_ref[...]
    q_low = q_unit.astype(BF16).astype(F32)

    own_meta = sent_ref[count + qcount :, :].astype(F32)
    before_meta = before[count + qcount :].astype(F32)
    columns = [own_meta[0:1, i : i + 1] for i in range(per_dev)]
    before_columns = [before_meta[0:1, i : i + 1] for i in range(per_dev)]
    grads = loss_grads(q_low, own_unit, after_unit, columns, per_dev, qtokens, pages)
    before_grads = loss_grads(before_q, before_rows, visit_unit, before_columns, per_dev, qtokens, pages)

    values = []
    for c in range(per_dev):
        for i in range(per_dev):
            values.append(grads[i][c] * q_low[i * qtokens : (i + 1) * qtokens])
        for i in range(per_dev):
            values.append(before_grads[i][per_dev + c] * before_q[i * qtokens : (i + 1) * qtokens])
    values = jnp.concatenate(values, axis=0)
    high = values.astype(BF16)
    rest = (values - high.astype(F32)).astype(BF16)
    parts = jnp.concatenate([high, rest], axis=1)
    values_ref[...] = parts
    both = jnp.dot(same_ref[...], parts, preferred_element_type=F32)
    wide = both[:, :width] + both[:, width:]
    unit = slot_unit_ref[...]
    out = (wide - unit * jnp.sum(unit * wide, axis=-1, keepdims=True)) * slot_inv_ref[...]

    low = []
    for i in range(per_dev):
        wide_q = jnp.zeros((qtokens, width), F32)
        for c in range(per_dev):
            start = (c * per_dev + i) * qtokens
            wide_q += grads[i][c] * own_unit[start : start + qtokens]
            wide_q += grads[i][per_dev + c] * after_unit[start : start + qtokens]
        unit_i = q_unit[i * qtokens : (i + 1) * qtokens]
        out_q = (wide_q - unit_i * jnp.sum(unit_i * wide_q, axis=-1, keepdims=True)) * q_inv[
            i * qtokens : (i + 1) * qtokens
        ]
        out_q = jnp.where(split == 0, out_q[:tokens], out_q[tokens:])
        d_query_ref[i] = out_q
        low.append(out_q)
    low = jnp.concatenate([out] + low, axis=0).astype(BF16)
    low_ref[...] = low
    send_ref[...] = partial_sum(there_ref, low).astype(BF16)


def page_kernel(values_ref, low_ref, here_ref, table_ref, unit_ref, inv_ref, query_ref, out_hbm, d_query_hbm, keep_ref, out_ref, sem):
    width = unit_ref.shape[1]
    small = pltpu.make_async_copy(query_ref, d_query_hbm, sem.at[0])
    small.start()
    both = jnp.dot(table_ref[...], values_ref[...], preferred_element_type=F32)
    wide = both[:, :width] + both[:, width:]
    unit = unit_ref[...]
    out = (wide - unit * jnp.sum(unit * wide, axis=-1, keepdims=True)) * inv_ref[...]
    out_ref[...] = out.reshape(out_ref.shape)
    copy = pltpu.make_async_copy(out_ref, out_hbm, sem.at[1])
    copy.start()
    keep_ref[...] = partial_sum(here_ref, low_ref[...])
    small.wait()
    copy.wait()


def add_kernel(keep_ref, got_ref, out_ref):
    for core, places in enumerate(exchange_order()[1]):

        @pl.when(lax.axis_index("core") == core)
        def _(places=places):
            for group, place in enumerate(places):
                out_ref[place] = (keep_ref[group] + got_ref[group].astype(F32)).astype(BF16)


def sum_kernel(parts_ref, out_ref):
    total = jnp.sum(parts_ref[...].astype(F32), axis=0)
    rows = out_ref.shape[0]
    out_ref[...] = total[:rows] + total[rows:]


def shards(page_hidden, query_hidden, page_pre, query_pre, match_index, positive):
    per_dev, patches_all, width = page_pre.shape
    qtokens = query_pre.shape[1]
    patches = page_hidden.shape[1]
    hidden = page_hidden.shape[2]
    groups = lax.axis_size(BLK)
    blocks = groups * 2
    pages = blocks * per_dev
    slots = per_dev * match_index.shape[1] * match_index.shape[2]
    page_t = jnp.transpose(page_pre, (1, 0, 2))
    hid_t = jnp.transpose(page_hidden, (1, 0, 2))
    limit = pltpu.CompilerParams(vmem_limit_bytes=24 * 2**20)
    place = pl.pallas_call(
        place_kernel,
        out_shape=jax.ShapeDtypeStruct((8, LANES), jnp.int32),
        out_specs=VMEM,
        compiler_params=limit,
        cost_estimate=pl.CostEstimate(flops=5 * 10**9, bytes_accessed=4096, transcendentals=0),
        name="place",
    )()
    count = slots // 2 + per_dev * qtokens + 16
    payload = jax.ShapeDtypeStruct((count, width), BF16)
    first, second, rows, half, misc = pl.pallas_call(
        functools.partial(gather_kernel, blocks),
        out_shape=(
            payload,
            payload,
            jax.ShapeDtypeStruct((slots, width), BF16),
            jax.ShapeDtypeStruct((patches, per_dev, width), BF16),
            jax.ShapeDtypeStruct((8, slots), jnp.int32),
        ),
        in_specs=[VMEM] * 5,
        out_specs=(VMEM,) * 5,
        compiler_params=limit,
        name="gather_rows",
    )(place, match_index, positive.reshape(1, per_dev), query_pre, page_t)
    swap = [(i, i ^ 1) for i in range(blocks)]
    cross = []
    for i in range(blocks):
        j = (i + 1) % blocks if i % 2 else (i - 1) % blocks
        for part in range(lax.axis_size("mp")):
            cross.append((2 * i + part, 2 * j + (part if i // (2 * RUN) == j // (2 * RUN) else 1 - part)))
    far = lax.ppermute(second, DP + ("mp",), cross)
    near = lax.ppermute(first, DP, swap)
    wide_rows = jax.ShapeDtypeStruct((patches * per_dev, width), F32)
    own_rows = jax.ShapeDtypeStruct((slots // 2, width), F32)
    own_queries = jax.ShapeDtypeStruct((per_dev * qtokens, width), F32)
    slot_rows = jax.ShapeDtypeStruct((slots, width), F32)
    share = hidden // (2 * groups)
    depth = slots + query_hidden.shape[0] * query_hidden.shape[1]
    by_core = jax.ShapeDtypeStruct((groups, share, depth), BF16)
    unit, inv, table, *local, here = pl.pallas_call(
        local_kernel,
        out_shape=(
            wide_rows,
            wide_rows,
            jax.ShapeDtypeStruct((patches * per_dev, slots), BF16),
            own_rows,
            own_rows,
            own_queries,
            own_queries,
            slot_rows,
            slot_rows,
            jax.ShapeDtypeStruct((slots, slots), BF16),
            by_core,
            by_core,
        ),
        in_specs=[VMEM] * 6,
        out_specs=(VMEM,) * 12,
        compiler_params=limit,
        cost_estimate=pl.CostEstimate(flops=5 * 10**9, bytes_accessed=10**6, transcendentals=0),
        name="local_rows",
    )(first, rows, half, misc, hid_t, query_hidden)
    d_query, values, low, send = pl.pallas_call(
        functools.partial(main_kernel, pages, per_dev),
        out_shape=(
            jax.ShapeDtypeStruct((per_dev, query_hidden.shape[1], width), F32),
            jax.ShapeDtypeStruct((slots, 2 * width), BF16),
            jax.ShapeDtypeStruct((depth, width), BF16),
            jax.ShapeDtypeStruct((groups, share, width), BF16),
        ),
        in_specs=[VMEM] * 11,
        out_specs=(VMEM,) * 4,
        compiler_params=limit,
        name="grads_and_partial",
    )(first, near, far, *local)
    got = lax.ppermute(send, "core", [(0, 1), (1, 0)])
    d_page, d_query, keep = pl.pallas_call(
        page_kernel,
        out_shape=(
            jax.ShapeDtypeStruct((patches, per_dev, width), F32),
            jax.ShapeDtypeStruct(d_query.shape, F32),
            jax.ShapeDtypeStruct((groups, share, width), F32),
        ),
        in_specs=[VMEM] * 7,
        out_specs=(ANY, ANY, VMEM),
        scratch_shapes=[pltpu.VMEM((patches, per_dev, width), F32), pltpu.SemaphoreType.DMA((2,))],
        compiler_params=limit,
        cost_estimate=pl.CostEstimate(flops=10**9, bytes_accessed=10**6, transcendentals=0),
        name="page_grads",
    )(values, low, here, table, unit, inv, d_query)
    small = pltpu.CompilerParams(vmem_limit_bytes=16 * 2**20)
    pair = pl.pallas_call(
        add_kernel,
        out_shape=jax.ShapeDtypeStruct(got.shape, BF16),
        in_specs=[VMEM, VMEM],
        out_specs=VMEM,
        compiler_params=small,
        name="add_pair",
    )(keep, got)
    parts = lax.all_to_all(
        pair.reshape(groups * 2, share // 2, width),
        DP + ("mp",),
        0,
        0,
        tiled=True,
        axis_index_groups=exchange_order()[0],
    )
    grad = pl.pallas_call(
        sum_kernel,
        out_shape=jax.ShapeDtypeStruct((share // 2, width), F32),
        in_specs=[VMEM],
        out_specs=VMEM,
        compiler_params=small,
        name="sum_parts",
    )(parts.reshape(groups, share, width))
    return jnp.transpose(d_page, (1, 0, 2)), d_query, grad


def solution(mesh):
    blocks, parts = mesh.devices.shape
    fine = Mesh(mesh.devices.reshape(2, 2, 2, blocks // 16, 2, parts), DP + ("mp",))
    placed = (
        P(DP, "mp", None),
        P(DP, "mp", None),
        P(DP, None, None),
        P(DP, None, None),
        P(DP, None, None),
        P(DP),
    )
    return jax.shard_map(
        shards,
        mesh=fine,
        in_specs=placed,
        out_specs=(P(DP, "mp", None), P(DP, "mp", None), P(DP + ("mp",), None)),
        check_vma=False,
    )
```
